128 devices in a mesh: dp: 4 (over z), seq: 32 (over x, y, core).
Axes of the slice: x: 4, y: 4, z: 4, core: 2. Of those that a mesh axis runs over, the one named last changes fastest.
Arguments:
- merged_product_embeddings: bfloat16 [65536, 4096], P(('dp', 'seq')), may hold values from -10 to 10
- fetched_home_chip: int32 [4, 32, 264, 1], P('dp', 'seq'), may hold values from 0 to 127; in each aligned block of 264 rows (0 to 263, 264 to 527, ..., all dimensions but the last counted through in order) at most 4 rows name the same one
- fetched_home_slot: int32 [4, 32, 264, 1], P('dp', 'seq'), may hold values from 0 to 511
- memory_fading_speeds: float32 [128, 32], P(('dp', 'seq')), may hold values from 0.00078125 to 0.0333333333
- forgetting_fraction: float32 [128, 256], P(('dp', 'seq')), may hold values from 0 to 0.5
- magnitude_scaling: float32 [4096], replicated, may hold values from 0.5 to 1.5
Outputs:
- row_loss: float32 [128, 256], P(('dp', 'seq'))
- user_grad: bfloat16 [128, 256, 4096], P(('dp', 'seq'))
- item_grad: float32 [65536, 4096], P(('dp', 'seq'))
The draws below stay inside these ranges and needn't reach their ends.
Inputs may be any that keep to these rules, and one draw needn't show every extreme that they name: `fetched_home_chip`: at most 4 of the 264 requests of one device name one owner; some owner receives exactly 4 from a device.
All inputs are finite; a program needn't handle non-finite values.
Results may differ from the reference program's by a relative error of at most 0.015.
Values may be sent and summed in bfloat16 or wider, within the bound.
No kernel may reach another device: no remote copies, remote signals or barrier semaphores. Data moves between devices by JAX's collectives and lax.ppermute only.
A program may use at most 128 MiB of HBM per device.

```python
import math
import jax
import jax.numpy as jnp
import numpy as np
from jax import lax

D = 4096
HEADS = 32
HEAD_DIM = 128
BEHAVIOUR_LENGTH = 256
ITEM_DEV = 512
NEG = 256
ROWS = 256
REQ = 264
CAP = 4
SHOPPERS_EACH_DP = 32
TOTAL_USERS = 128
ITEMS = 65536
N_DP = 4
N_SEQ = 32


def draw_merged_product_embeddings(key, part):
    key = jax.random.fold_in(key, 37)
    noise_key = jax.random.fold_in(key, 0)
    noise = jax.random.normal(noise_key, (ITEMS, D), jnp.float32)
    value = jnp.clip(noise, -6.0, 6.0)
    return value.astype(jnp.bfloat16)


def draw_memory_fading_speeds(key, part):
    key = jax.random.fold_in(key, 11)
    pick_key, spread = jax.random.split(key)
    fast_share = 0.5
    fast_heads = jax.random.uniform(pick_key, (TOTAL_USERS, HEADS), jnp.float32) < fast_share
    uniform_level = jax.random.uniform(spread, (TOTAL_USERS, HEADS), jnp.float32)
    fast_rate = jnp.exp(jnp.log(1.0 / 50.0) + uniform_level * (jnp.log(1.0 / 30.0) - jnp.log(1.0 / 50.0)))
    slow_rate = (0.2 + 0.8 * uniform_level) / BEHAVIOUR_LENGTH
    return jnp.where(fast_heads, fast_rate, slow_rate).astype(jnp.float32)


def draw_forgetting_fraction(key, part):
    key = jax.random.fold_in(key, 23)
    location_random_key, amount_random_key = jax.random.split(key)
    local_spike = jax.random.uniform(location_random_key, (TOTAL_USERS, BEHAVIOUR_LENGTH), jnp.float32) < 3.0 / BEHAVIOUR_LENGTH
    spike_length = 0.2 + 0.3 * jax.random.uniform(amount_random_key, (TOTAL_USERS, BEHAVIOUR_LENGTH), jnp.float32)
    return jnp.where(local_spike, spike_length, 0.0).astype(jnp.float32)


def touch_ends(entries, own_key, low, top_value):
    longest = entries.shape.index(max(entries.shape))
    spots = []
    for shift in (0, 1):
        where = [jax.random.randint(jax.random.fold_in(own_key, axis), (), 0, length) for axis, length in enumerate(entries.shape)]
        where[longest] = (where[longest] + shift) % entries.shape[longest]
        spots.append(tuple(where))
    return entries.at[spots[0]].set(low).at[spots[1]].set(top_value)


def cumulative_ranks(count, skew):
    loads = [(1 << 20) // math.isqrt(standing ** skew) + 1 for standing in range(1, count + 1)]
    scale = 1 + sum(loads) // (1 << 30)
    return np.cumsum(np.array([max(1, weight // scale) for weight in loads]))


def ranked_ids(stream_key, shape, number_of, skew):
    table = cumulative_ranks(number_of, skew)
    pick = jax.random.randint(jax.random.fold_in(stream_key, 1), shape, 0, int(table[number_of - 1]))
    grade = jnp.searchsorted(jnp.asarray(table, jnp.int32), pick, side="right")
    return jax.random.permutation(jax.random.fold_in(stream_key, 2), number_of)[grade].astype(jnp.int32)


def routed_block(own_key, own, number, rows, amount, top, bound, slope):
    order = jax.random.permutation(own_key, amount)
    packed, usual = portions_of(amount, rows * top, bound, slope, True), portions_of(amount, rows * top, bound, slope, False)
    places = jnp.arange(amount)

    def named(lengths, offset_by):
        used = int((lengths > 0).sum())
        fixed = max(1, used // 4)
        passed = fixed + (places - fixed + offset_by * (used - fixed)) % max(1, amount - fixed)
        return jnp.zeros((amount,), jnp.int32).at[order[jnp.where(places < fixed, places, passed)]].set(jnp.asarray(lengths, jnp.int32))

    lengths = jnp.where(number % 4 == 0, named(packed, number // 4), named(usual, number - number // 4 - 1))
    mixed = jax.random.permutation(jax.random.fold_in(own, 3), amount)
    giver, sink = mixed[0:amount // 2 * 2:2], mixed[1:amount // 2 * 2:2]
    slack = jnp.minimum(lengths[giver] - 1, bound - lengths[sink]) // 2
    slack = jnp.where((giver == order[0]) | (sink == order[0]) | (lengths[sink] == 0), 0, jnp.maximum(slack, 0))
    passed = jax.random.randint(jax.random.fold_in(own, 4), (amount // 2,), 0, 1 << 20) % (slack + 1)
    lengths = lengths.at[giver].add(-passed).at[sink].add(passed)
    members = jnp.searchsorted(jnp.cumsum(lengths), jnp.arange(rows * top), side="right").astype(jnp.int32)
    grid = members.reshape(top, rows).T
    grid = grid[jax.random.permutation(jax.random.fold_in(own, 1), rows)]
    offset_by = jax.random.randint(jax.random.fold_in(own, 2), (rows, 1), 0, top)
    return jnp.take_along_axis(grid, (jnp.arange(top)[None, :] + offset_by) % top, axis=1)


def portions_of(count, total, limit, slope, full):
    portions = [(1 << 20) // math.isqrt(grade ** slope) + 1 for grade in range(1, count + 1)]
    largest = limit if full else min(limit, max(-(-total // count), total * portions[0] // sum(portions)))
    least = 1 if total - largest >= count - 1 else 0
    given, spare = [largest] + [least] * (count - 1), total - largest - least * (count - 1)
    while spare > 0:
        free = [i for i in range(1, count) if given[i] < largest] or [i for i in range(1, count) if given[i] < limit]
        whole, left = sum([portions[i] for i in free]), spare
        for i in free:
            addition = min(limit - given[i], max(1, left * portions[i] // whole), spare)
            given[i] = given[i] + addition
            spare = spare - addition
    return np.array(given)


def setup_inputs(seed: int = 0) -> dict:
    splits = jax.random.split(jax.random.key(seed), 7)
    merged_product_embeddings = draw_merged_product_embeddings(jax.random.fold_in(splits[6], 71), 0)
    fetched_home_chip_keys = jax.random.split(jax.random.fold_in(splits[1], 1), N_DP * N_SEQ * REQ // REQ)
    fetched_home_chip_turns = jax.random.permutation(jax.random.fold_in(splits[1], 3), N_DP * N_SEQ * REQ // REQ)
    fetched_home_chip = jax.vmap(lambda own, number: routed_block(jax.random.fold_in(splits[1], 2), own, number, REQ, N_DP * N_SEQ, 1, CAP, 1))(fetched_home_chip_keys, fetched_home_chip_turns).reshape((N_DP, N_SEQ, REQ, 1))
    fetched_home_slot = touch_ends(ranked_ids(splits[2], (N_DP, N_SEQ, REQ, 1), ITEM_DEV, 2), jax.random.fold_in(splits[2], 3), 0, ITEM_DEV - 1).astype(jnp.int32)
    memory_fading_speeds = draw_memory_fading_speeds(jax.random.fold_in(splits[6], 71), 0)
    forgetting_fraction = draw_forgetting_fraction(jax.random.fold_in(splits[6], 71), 0)
    magnitude_scaling = jnp.clip(1.0 + 0.1 * jax.random.normal(splits[5], (D,), jnp.float32), 0.5, 1.5)
    return dict(merged_product_embeddings=merged_product_embeddings, fetched_home_chip=fetched_home_chip, fetched_home_slot=fetched_home_slot, memory_fading_speeds=memory_fading_speeds, forgetting_fraction=forgetting_fraction, magnitude_scaling=magnitude_scaling)


def reference(merged_product_embeddings, fetched_home_chip, fetched_home_slot, memory_fading_speeds, forgetting_fraction, magnitude_scaling):
    score_scale = 4.0 / math.sqrt(D)
    item_ids = (fetched_home_chip[..., 0] * ITEM_DEV + fetched_home_slot[..., 0]).astype(jnp.int32)
    valid_mask = jnp.tile((jnp.arange(BEHAVIOUR_LENGTH, dtype=jnp.int32) > 0).astype(jnp.float32), SHOPPERS_EACH_DP)

    def one_group(gradient_sum, feature_band):
        group_ids = lax.dynamic_index_in_dim(item_ids, feature_band, 0, keepdims=False)
        behaviour_ids = group_ids[:, :ROWS].reshape(SHOPPERS_EACH_DP, BEHAVIOUR_LENGTH)
        negative_ids = group_ids[:, ROWS:].reshape(NEG)
        behaviour_rows = merged_product_embeddings[behaviour_ids]
        negatives = merged_product_embeddings[negative_ids]
        decay_values = lax.dynamic_slice_in_dim(memory_fading_speeds, (feature_band * SHOPPERS_EACH_DP).astype(jnp.int32), SHOPPERS_EACH_DP, 0)
        impulse_series = lax.dynamic_slice_in_dim(forgetting_fraction, (feature_band * SHOPPERS_EACH_DP).astype(jnp.int32), SHOPPERS_EACH_DP, 0)

        def advance(running, sequence_position):
            current = lax.dynamic_index_in_dim(behaviour_rows, sequence_position, 1, keepdims=False)
            current = current.astype(jnp.float32).reshape(SHOPPERS_EACH_DP, HEADS, HEAD_DIM)
            present_spike = lax.dynamic_index_in_dim(impulse_series, sequence_position, 1, keepdims=False)
            fading_factor = jnp.exp(-decay_values) * (1.0 - present_spike)[:, None]
            return (fading_factor[:, :, None] * running + current, running.reshape(SHOPPERS_EACH_DP, D))
        _, priors = lax.scan(advance, jnp.zeros((SHOPPERS_EACH_DP, HEADS, HEAD_DIM), jnp.float32), jnp.arange(BEHAVIOUR_LENGTH, dtype=jnp.int32))
        prior_state = jnp.transpose(priors, (1, 0, 2)).reshape(SHOPPERS_EACH_DP * BEHAVIOUR_LENGTH, D)
        norm_factor = lax.rsqrt(lax.optimization_barrier(jnp.mean(prior_state * prior_state, axis=1, keepdims=True)) + 1e-06)
        user_rep = (prior_state * norm_factor * magnitude_scaling[None, :]).astype(jnp.bfloat16)
        flat_rows = behaviour_rows.reshape(SHOPPERS_EACH_DP * BEHAVIOUR_LENGTH, D)
        pos_logit = score_scale * lax.optimization_barrier(jnp.sum(user_rep.astype(jnp.float32) * flat_rows.astype(jnp.float32), axis=1))
        neg_logit = score_scale * jnp.dot(user_rep, negatives.T, preferred_element_type=jnp.float32)
        row_max = jnp.maximum(lax.optimization_barrier(jnp.max(neg_logit, axis=1)), pos_logit)
        row_total = jnp.exp(pos_logit - row_max) + lax.optimization_barrier(jnp.sum(jnp.exp(neg_logit - row_max[:, None]), axis=1))
        log_total = row_max + jnp.log(row_total)
        row_loss = (log_total - pos_logit) * valid_mask
        d_pos = (jnp.exp(pos_logit - log_total) - 1.0) * valid_mask
        d_neg = (jnp.exp(neg_logit - log_total[:, None]) * valid_mask[:, None]).astype(jnp.bfloat16)
        user_grad = score_scale * (d_pos[:, None] * flat_rows.astype(jnp.float32) + jnp.dot(d_neg, negatives, preferred_element_type=jnp.float32))
        user_grad = user_grad.astype(jnp.bfloat16)
        pos_grad = score_scale * d_pos[:, None] * user_rep.astype(jnp.float32)
        neg_grad = score_scale * jnp.dot(d_neg.T, user_rep, preferred_element_type=jnp.float32)
        gradient_sum = gradient_sum.at[behaviour_ids.reshape(-1)].add(pos_grad).at[negative_ids].add(neg_grad)
        return (gradient_sum, (row_loss.reshape(SHOPPERS_EACH_DP, BEHAVIOUR_LENGTH), user_grad.reshape(SHOPPERS_EACH_DP, BEHAVIOUR_LENGTH, D)))
    gradient_sum, (losses, user_grads) = lax.scan(one_group, jnp.zeros((ITEMS, D), jnp.float32), jnp.arange(N_DP, dtype=jnp.int32))
    return (losses.reshape(TOTAL_USERS, BEHAVIOUR_LENGTH), user_grads.reshape(TOTAL_USERS, BEHAVIOUR_LENGTH, D), gradient_sum)
```

```python
import functools

import jax
import jax.numpy as jnp
from jax import lax
from jax.experimental import pallas as pl
from jax.experimental.pallas import tpu as pltpu
from jax.sharding import PartitionSpec as P

D = 4096
HEADS = 32
HEAD_DIM = 128
STEPS = 256
OWN_NEG = 8
REQ = STEPS + OWN_NEG
NEG = 256
ITEMS = 512
DEVICES = 128
CAP = 4
SLOTS = DEVICES * CAP
SIGMA = 4.0 / 64.0
BLOCK = 1024
F32 = jnp.float32
BF16 = jnp.bfloat16
I32 = jnp.int32
AXES = ("dp", "seq")
PARAMS = pltpu.CompilerParams(vmem_limit_bytes=48 * 2**20)


def iota(shape, dim):
    return lax.broadcasted_iota(I32, shape, dim)


def call(kernel, out_shape, name, **kw):
    return pl.pallas_call(kernel, out_shape=out_shape, name=name, compiler_params=PARAMS, **kw)


def matmul(a, b, dims):
    return lax.dot_general(a, b, ((dims[0], dims[1]), ((), ())), preferred_element_type=F32)


def route_kernel(owner_col, owner_row, item_row, wanted, slots):
    col, row = owner_col[...], owner_row[...]

    def key(i):
        return jnp.where(i >= STEPS, i - 2 * STEPS, i)

    earlier = key(iota((REQ, REQ), 0)) < key(iota((REQ, REQ), 1))
    rank = jnp.sum(jnp.where((col == row) & earlier, 1.0, 0.0), axis=0, keepdims=True).astype(I32)
    slots[...] = row * CAP + rank
    item = (item_row[...] + 1).astype(F32)
    here = iota((DEVICES, REQ), 0) == row
    out = jnp.full((DEVICES, 128), -1.0, F32)
    lane = iota((DEVICES, 128), 1)
    for s in range(CAP):
        named = jnp.sum(jnp.where(here & (rank == s), item, 0.0), axis=1, keepdims=True)
        out = jnp.where(lane == s, named - 1.0, out)
    wanted[...] = out.astype(I32)


def onehot_items(asked):
    asked = asked.astype(F32)
    device, slot = iota((DEVICES, SLOTS), 0), iota((DEVICES, SLOTS), 1)
    row = jnp.zeros((DEVICES, SLOTS), F32)
    for s in range(CAP):
        row = row + jnp.where(slot == device * CAP + s, asked[:, s : s + 1], 0.0)
    row = jnp.sum(row, axis=0, keepdims=True)
    return (iota((ITEMS, SLOTS), 0).astype(F32) == row).astype(F32).astype(BF16)


def pick_kernel(asked, table, out, hot):
    @pl.when(pl.program_id(0) == 0)
    def _():
        hot[...] = onehot_items(asked[...])

    rows = matmul(hot[...], table[...], ((0,), (0,)))
    out[...] = rows.astype(BF16).reshape(out.shape)


def place_kernel(asked, arrived, out, hot):
    @pl.when(pl.program_id(0) == 0)
    def _():
        hot[...] = onehot_items(asked[...])

    out[...] = matmul(hot[...], arrived[...].reshape(SLOTS, arrived.shape[2]), ((1,), (0,)))


def onehot_slots(slots):
    return (iota((SLOTS, slots.shape[1]), 0) == slots).astype(F32).astype(BF16)


def own_negatives_kernel(slots, rows, out):
    hot = onehot_slots(slots[:, STEPS:REQ])
    out[...] = matmul(hot, rows[...].reshape(SLOTS, rows.shape[2]), ((0,), (0,))).astype(BF16)


def decay_kernel(speeds, forget_row, forget_col, out, base):
    step, source = iota((STEPS, STEPS), 0), iota((STEPS, STEPS), 1)

    @pl.when(pl.program_id(0) == 0)
    def _():
        log_row, log_col = jnp.log(1.0 - forget_row[...]), jnp.log(1.0 - forget_col[...])
        until = jnp.sum(jnp.where(source < step, log_row, 0.0), axis=1, keepdims=True)
        through = jnp.sum(jnp.where(step <= source, log_col, 0.0), axis=0, keepdims=True)
        base[...] = jnp.where(source < step, until - through, -1e30)

    span = (step - 1 - source).astype(F32)
    for k in range(out.shape[0]):
        speed = speeds[0, pl.program_id(0) * out.shape[0] + k]
        full = jnp.exp(base[...] - speed * span)
        high = full.astype(BF16)
        out[k, :, :STEPS] = high
        out[k, :, STEPS:] = (full - high.astype(F32)).astype(BF16)


def state_kernel(slots, rows, decay, gain, x_out, rep_out, pos_out, hot, prior, total):
    j, last = pl.program_id(0), pl.num_programs(0) - 1
    width = rows.shape[2]

    @pl.when(j == 0)
    def _():
        hot[...] = onehot_slots(slots[:, :STEPS])
        total[...] = jnp.zeros_like(total)

    x = matmul(hot[...], rows[...].reshape(SLOTS, width), ((0,), (0,))).astype(BF16)
    columns = pl.ds(pl.multiple_of(j * width, width), width)
    x_out[:, columns] = x
    for k in range(width // HEAD_DIM):
        part = slice(k * HEAD_DIM, (k + 1) * HEAD_DIM)
        xk = x[:, part]
        state = matmul(decay[k, :, :STEPS], xk, ((1,), (0,))) + matmul(
            decay[k, :, STEPS:], xk, ((1,), (0,))
        )
        total[...] += state * state
        prior[:, pl.ds(pl.multiple_of(j * width + k * HEAD_DIM, HEAD_DIM), HEAD_DIM)] = state

    @pl.when(j == last)
    def _():
        norm = lax.rsqrt(jnp.sum(total[...], axis=1, keepdims=True) * (1.0 / D) + 1e-06)
        pos = jnp.zeros((STEPS, HEAD_DIM), F32)
        for c in range(0, D, HEAD_DIM):
            part = slice(c, c + HEAD_DIM)
            rep = (prior[:, part] * norm * gain[:, part]).astype(BF16)
            rep_out[:, part] = rep
            pos = pos + rep.astype(F32) * x_out[:, part].astype(F32)
        pos_out[...] = SIGMA * jnp.sum(pos, axis=1, keepdims=True)


def loss_kernel(rep, near, far, pos_logit, loss, d_pos, d_neg, neg_part):
    u = rep[...]
    half = NEG // 2
    logits = [SIGMA * matmul(u, n[...], ((1,), (1,))) for n in (near, far)]
    pos = pos_logit[...]
    top = jnp.maximum(jnp.max(jnp.maximum(*logits), axis=1, keepdims=True), pos)
    summed = sum(jnp.sum(jnp.exp(l - top), axis=1, keepdims=True) for l in logits)
    log_total = top + jnp.log(jnp.exp(pos - top) + summed)
    valid = jnp.where(iota((STEPS, 1), 0) > 0, 1.0, 0.0)
    loss[...] = (log_total - pos) * valid
    d_pos[...] = (jnp.exp(pos - log_total) - 1.0) * valid
    for k, l in enumerate(logits):
        share = (jnp.exp(l - log_total) * valid).astype(BF16)
        d_neg[:, k * half : (k + 1) * half] = share
        neg_part[k * half : (k + 1) * half, :] = (SIGMA * matmul(share, u, ((0,), (0,)))).astype(BF16)


def outgoing_kernel(slots, rep, d_pos, neg_grad, out, hot, hot_neg):
    @pl.when(pl.program_id(0) == 0)
    def _():
        hot[...] = onehot_slots(slots[:, :STEPS])
        hot_neg[...] = onehot_slots(slots[:, STEPS:REQ])

    grad = (SIGMA * d_pos[...] * rep[...].astype(F32)).astype(BF16)
    rows = matmul(hot[...], grad, ((1,), (0,))) + matmul(hot_neg[...], neg_grad[...], ((1,), (0,)))
    out[...] = rows.astype(BF16).reshape(out.shape)


def user_grad_kernel(x, d_pos, d_neg, near, far, out):
    half = NEG // 2
    from_neg = matmul(d_neg[:, :half], near[...], ((1,), (0,))) + matmul(
        d_neg[:, half:], far[...], ((1,), (0,))
    )
    out[0] = (SIGMA * (d_pos[...] * x[...].astype(F32) + from_neg)).astype(BF16)


def shift(value, dx=0, dy=0, core=0):
    pairs = []
    for x in range(4):
        for y in range(4):
            for c in range(2):
                to = ((x + dx) % 4 * 4 + (y + dy) % 4) * 2 + (c ^ core)
                pairs.append(((x * 4 + y) * 2 + c, to))
    return lax.ppermute(value, "seq", pairs)


def spread_negatives(own):
    line = jnp.concatenate([own] + [shift(own, dy=k) for k in (1, 2, 3)], axis=0)
    near = jnp.concatenate([line] + [shift(line, dx=k) for k in (1, 2, 3)], axis=0)
    return near, shift(near, core=1)


def add(parts):
    return sum(p.astype(F32) for p in parts).astype(BF16)


def collect_negatives(part):
    half = NEG // 2
    plane = add([part[:half], shift(part[half:], core=1)])
    n = half // 4
    line = add([plane[:n]] + [shift(plane[k * n : (k + 1) * n], dx=-k) for k in (1, 2, 3)])
    n = n // 4
    return add([line[:n]] + [shift(line[k * n : (k + 1) * n], dy=-k) for k in (1, 2, 3)])


def exchange(rows):
    return lax.all_to_all(rows, AXES, split_axis=0, concat_axis=0, tiled=True)


def whole(shape):
    return pl.BlockSpec(shape, lambda j: (0,) * len(shape))


def on_device(table, home, item, speeds, forget, gain):
    grid = (D // BLOCK,)
    columns = lambda n: pl.BlockSpec((n, BLOCK), lambda j: (0, j))
    slots_block = pl.BlockSpec((DEVICES, CAP, BLOCK), lambda j: (0, 0, j))
    shape = jax.ShapeDtypeStruct
    wanted, slots = call(
        route_kernel, (shape((DEVICES, 128), I32), shape((1, REQ), I32)), "route"
    )(home.reshape(REQ, 1), home.reshape(1, REQ), item.reshape(1, REQ))
    asked = exchange(wanted.reshape(DEVICES, 1, 128)).reshape(DEVICES, 128)
    picked = call(
        pick_kernel,
        shape((DEVICES, CAP, D), BF16),
        "pick",
        grid=grid,
        in_specs=[whole((DEVICES, 128)), columns(ITEMS)],
        out_specs=slots_block,
        scratch_shapes=[pltpu.VMEM((ITEMS, SLOTS), BF16)],
    )(asked, table)
    fetched = exchange(picked)
    group = 4
    decay = call(
        decay_kernel,
        shape((HEADS, STEPS, 2 * STEPS), BF16),
        "decay",
        grid=(HEADS // group,),
        in_specs=[
            pl.BlockSpec(memory_space=pltpu.SMEM),
            whole((1, STEPS)),
            whole((STEPS, 1)),
        ],
        out_specs=pl.BlockSpec((group, STEPS, 2 * STEPS), lambda j: (j, 0, 0)),
        scratch_shapes=[pltpu.VMEM((STEPS, STEPS), F32)],
    )(speeds, forget, forget.reshape(STEPS, 1))
    own = call(
        own_negatives_kernel,
        shape((OWN_NEG, D), BF16),
        "own_negatives",
        grid=grid,
        in_specs=[whole((1, REQ)), slots_block],
        out_specs=columns(OWN_NEG),
    )(slots, fetched)
    near, far = spread_negatives(own)
    x, rep, pos_logit = call(
        state_kernel,
        (shape((STEPS, D), BF16), shape((STEPS, D), BF16), shape((STEPS, 1), F32)),
        "state",
        grid=grid,
        in_specs=[
            whole((1, REQ)),
            slots_block,
            pl.BlockSpec((BLOCK // HEAD_DIM, STEPS, 2 * STEPS), lambda j: (j, 0, 0)),
            whole((1, D)),
        ],
        out_specs=(whole((STEPS, D)), whole((STEPS, D)), whole((STEPS, 1))),
        scratch_shapes=[
            pltpu.VMEM((SLOTS, STEPS), BF16),
            pltpu.VMEM((STEPS, D), F32),
            pltpu.VMEM((STEPS, HEAD_DIM), F32),
        ],
    )(slots, fetched, decay, gain.reshape(1, D))
    loss, d_pos, d_neg, neg_part = call(
        loss_kernel,
        (
            shape((STEPS, 1), F32),
            shape((STEPS, 1), F32),
            shape((STEPS, NEG), BF16),
            shape((NEG, D), BF16),
        ),
        "loss",
    )(rep, near, far, pos_logit)
    neg_grad = collect_negatives(neg_part)
    outgoing = call(
        outgoing_kernel,
        shape((DEVICES, CAP, D), BF16),
        "outgoing",
        grid=grid,
        in_specs=[whole((1, REQ)), columns(STEPS), whole((STEPS, 1)), columns(OWN_NEG)],
        out_specs=slots_block,
        scratch_shapes=[pltpu.VMEM((SLOTS, STEPS), BF16), pltpu.VMEM((SLOTS, OWN_NEG), BF16)],
    )(slots, rep, d_pos, neg_grad)
    arrived = exchange(outgoing)
    user_grad = call(
        user_grad_kernel,
        shape((1, STEPS, D), BF16),
        "user_grad",
        grid=grid,
        in_specs=[
            columns(STEPS),
            whole((STEPS, 1)),
            whole((STEPS, NEG)),
            columns(NEG // 2),
            columns(NEG // 2),
        ],
        out_specs=pl.BlockSpec((1, STEPS, BLOCK), lambda j: (0, 0, j)),
    )(x, d_pos, d_neg, near, far)
    item_grad = call(
        place_kernel,
        shape((ITEMS, D), F32),
        "place",
        grid=grid,
        in_specs=[whole((DEVICES, 128)), slots_block],
        out_specs=columns(ITEMS),
        scratch_shapes=[pltpu.VMEM((ITEMS, SLOTS), BF16)],
    )(asked, arrived)
    return loss.reshape(1, STEPS), user_grad, item_grad


def solution(mesh):
    return jax.shard_map(
        on_device,
        mesh=mesh,
        in_specs=(
            P(AXES, None),
            P("dp", "seq", None, None),
            P("dp", "seq", None, None),
            P(AXES, None),
            P(AXES, None),
            P(),
        ),
        out_specs=(P(AXES, None), P(AXES, None, None), P(AXES, None)),
        check_vma=False,
    )
```

```python
import jax
import jax.numpy as jnp
from jax import lax
from jax.experimental import pallas as pl
from jax.experimental.pallas import tpu as pltpu
from jax.sharding import PartitionSpec as P

D = 4096
HEADS = 32
HEAD_DIM = 128
STEPS = 256
OWN_NEG = 8
REQ = STEPS + OWN_NEG
NEG = 256
ITEMS = 512
DEVICES = 128
CAP = 4
SLOTS = DEVICES * CAP
SIGMA = 4.0 / 64.0
BLOCK = dict(pick=1024, state=1024, base=1024, user_grad=1024, place=1024)
F32 = jnp.float32
BF16 = jnp.bfloat16
I32 = jnp.int32
AXES = ("dp", "seq")


def iota(shape, dim):
    return lax.broadcasted_iota(I32, shape, dim)


def call(kernel, out_shape, name, cost=None, vmem=60, **kw):
    if cost is not None:
        flops, size = cost
        kw["cost_estimate"] = pl.CostEstimate(flops=flops, bytes_accessed=size, transcendentals=0)
    params = pltpu.CompilerParams(vmem_limit_bytes=vmem * 2**20)
    return pl.pallas_call(kernel, out_shape=out_shape, name=name, compiler_params=params, **kw)


def matmul(a, b, dims):
    return lax.dot_general(a, b, ((dims[0], dims[1]), ((), ())), preferred_element_type=F32)


def route_kernel(owner_row, item_row, wanted, slots):
    row = owner_row[...]
    same = iota((REQ, REQ), 0) == iota((REQ, REQ), 1)
    col = jnp.sum(jnp.where(same, row.astype(F32), 0.0), axis=1, keepdims=True).astype(I32)

    def key(i):
        return jnp.where(i >= STEPS, i - 2 * STEPS, i)

    earlier = key(iota((REQ, REQ), 0)) < key(iota((REQ, REQ), 1))
    rank = jnp.sum(jnp.where((col == row) & earlier, 1.0, 0.0), axis=0, keepdims=True).astype(I32)
    slots[...] = row * CAP + rank
    item = (item_row[...] + 1).astype(F32)
    here = iota((DEVICES, REQ), 0) == row
    lane = iota((DEVICES, 128), 1)
    out = jnp.full((DEVICES, 128), -1.0, F32)
    for s in range(CAP):
        named = jnp.sum(jnp.where(here & (rank == s), item, 0.0), axis=1, keepdims=True)
        out = jnp.where(lane == s, named - 1.0, out)
    wanted[...] = out.astype(I32)


def onehot_items(asked):
    asked = asked.astype(F32)
    device, slot = iota((DEVICES, SLOTS), 0), iota((DEVICES, SLOTS), 1)
    row = jnp.zeros((DEVICES, SLOTS), F32)
    for s in range(CAP):
        row = row + jnp.where(slot == device * CAP + s, asked[:, s : s + 1], 0.0)
    row = jnp.sum(row, axis=0, keepdims=True)
    return (iota((ITEMS, SLOTS), 0).astype(F32) == row).astype(F32).astype(BF16)


def pick_kernel(asked, table, out, hot):
    @pl.when(pl.program_id(0) == 0)
    def _():
        hot[...] = onehot_items(asked[...])

    rows = matmul(hot[...], table[...], ((0,), (0,)))
    out[...] = rows.astype(BF16).reshape(out.shape)


def marks_kernel(asked, hot):
    hot[...] = onehot_items(asked[...])


def place_kernel(hot, arrived, out):
    out[...] = matmul(hot[...], arrived[...].reshape(SLOTS, out.shape[1]), ((1,), (0,)))


def onehot_slots(slots):
    return (iota((SLOTS, slots.shape[1]), 0) == slots).astype(F32).astype(BF16)


def own_negatives_kernel(slots, rows, out, held, sems):
    copies = []
    for k in range(OWN_NEG):
        owner = slots[0, STEPS + k] // CAP
        copies.append(pltpu.make_async_copy(rows.at[owner], held.at[k], sems.at[k]))
        copies[-1].start()
    total = jnp.zeros(out.shape, F32)
    for k in range(OWN_NEG):
        copies[k].wait()
        rank = slots[0, STEPS + k] % CAP
        tile = jnp.where(iota((CAP, D), 0) == rank, held[k].astype(F32), 0.0)
        row = jnp.sum(tile, axis=0, keepdims=True)
        total = jnp.where(iota(out.shape, 0) == k, row, total)
    out[...] = total.astype(BF16)


def decay_kernel(speeds, forget_row, forget_col, out, base):
    step, source = iota((STEPS, STEPS), 0), iota((STEPS, STEPS), 1)

    @pl.when(pl.program_id(0) == 0)
    def _():
        log_row, log_col = jnp.log(1.0 - forget_row[...]), jnp.log(1.0 - forget_col[...])
        until = jnp.sum(jnp.where(source < step, log_row, 0.0), axis=1, keepdims=True)
        through = jnp.sum(jnp.where(step <= source, log_col, 0.0), axis=0, keepdims=True)
        base[...] = jnp.where(source < step, until - through, -1e30)

    span = (step - 1 - source).astype(F32)
    for k in range(out.shape[0]):
        speed = speeds[0, pl.program_id(0) * out.shape[0] + k]
        full = jnp.exp(base[...] - speed * span)
        high = full.astype(BF16)
        out[k, :, :STEPS] = high
        out[k, :, STEPS:] = (full - high.astype(F32)).astype(BF16)


def state_kernel(slots, rows, decay, gain, x_out, rep_out, pos_out, hot, prior, total):
    j, last = pl.program_id(0), pl.num_programs(0) - 1
    width = rows.shape[2]

    @pl.when(j == 0)
    def _():
        hot[...] = onehot_slots(slots[:, :STEPS])
        total[...] = jnp.zeros_like(total)

    x = matmul(hot[...], rows[...].reshape(SLOTS, width), ((0,), (0,))).astype(BF16)
    columns = pl.ds(pl.multiple_of(j * width, width), width)
    x_out[:, columns] = x
    for k in range(width // HEAD_DIM):
        part = slice(k * HEAD_DIM, (k + 1) * HEAD_DIM)
        xk = x[:, part]
        state = matmul(decay[k, :, :STEPS], xk, ((1,), (0,))) + matmul(
            decay[k, :, STEPS:], xk, ((1,), (0,))
        )
        total[...] += state * state
        prior[:, pl.ds(pl.multiple_of(j * width + k * HEAD_DIM, HEAD_DIM), HEAD_DIM)] = state

    @pl.when(j == last)
    def _():
        norm = lax.rsqrt(jnp.sum(total[...], axis=1, keepdims=True) * (1.0 / D) + 1e-06)
        pos = jnp.zeros((STEPS, HEAD_DIM), F32)
        for c in range(0, D, HEAD_DIM):
            part = slice(c, c + HEAD_DIM)
            rep = (prior[:, part] * norm * gain[:, part]).astype(BF16)
            rep_out[:, part] = rep
            pos = pos + rep.astype(F32) * x_out[:, part].astype(F32)
        pos_out[...] = SIGMA * jnp.sum(pos, axis=1, keepdims=True)


def loss_kernel(rep, near, far, pos_logit, loss, d_pos, d_neg, near_part, far_part):
    u = rep[...]
    half = NEG // 2
    logits = [SIGMA * matmul(u, n[...], ((1,), (1,))) for n in (near, far)]
    pos = pos_logit[...]
    top = jnp.maximum(jnp.max(jnp.maximum(*logits), axis=1, keepdims=True), pos)
    summed = sum(jnp.sum(jnp.exp(l - top), axis=1, keepdims=True) for l in logits)
    log_total = top + jnp.log(jnp.exp(pos - top) + summed)
    valid = jnp.where(iota((STEPS, 1), 0) > 0, 1.0, 0.0)
    loss[...] = (log_total - pos) * valid
    d_pos[...] = (jnp.exp(pos - log_total) - 1.0) * valid
    for k, (l, part) in enumerate(zip(logits, (near_part, far_part))):
        share = (jnp.exp(l - log_total) * valid).astype(BF16)
        d_neg[:, k * half : (k + 1) * half] = share
        part[...] = (SIGMA * matmul(share, u, ((0,), (0,)))).astype(BF16)


def base_kernel(slots, rep, d_pos, out, hot):
    @pl.when(pl.program_id(0) == 0)
    def _():
        hot[...] = onehot_slots(slots[:, :STEPS])

    grad = (SIGMA * d_pos[...] * rep[...].astype(F32)).astype(BF16)
    out[...] = matmul(hot[...], grad, ((1,), (0,))).astype(BF16).reshape(out.shape)


def insert_kernel(slots, base, *refs):
    *parts, out, held, sems = refs
    owners = [slots[0, STEPS + k] // CAP for k in range(OWN_NEG)]
    reads = [
        pltpu.make_async_copy(base.at[owners[k]], held.at[k], sems.at[k]) for k in range(OWN_NEG)
    ]
    for copy in reads:
        copy.start()
    total = sum(p[...].astype(F32) for p in parts)
    for copy in reads:
        copy.wait()
    firsts = []
    for k in range(OWN_NEG):
        first = jnp.int32(k)
        for j in reversed(range(k)):
            first = jnp.where(owners[j] == owners[k], j, first)
        firsts.append(first)
        rank = slots[0, STEPS + k] % CAP
        tile = jnp.where(iota((CAP, D), 0) == rank, total[k : k + 1], held[first].astype(F32))
        held[first] = tile.astype(BF16)
    writes = [
        pltpu.make_async_copy(held.at[k], out.at[owners[k]], sems.at[k]) for k in range(OWN_NEG)
    ]
    for k, copy in enumerate(writes):
        pl.when(firsts[k] == k)(copy.start)
    for k, copy in enumerate(writes):
        pl.when(firsts[k] == k)(copy.wait)


def user_grad_kernel(x, d_pos, d_neg, near, far, out):
    half = NEG // 2
    from_neg = matmul(d_neg[:, :half], near[...], ((1,), (0,))) + matmul(
        d_neg[:, half:], far[...], ((1,), (0,))
    )
    out[0] = (SIGMA * (d_pos[...] * x[...].astype(F32) + from_neg)).astype(BF16)


def turn(value, stage, by):
    pairs = []
    for x in range(4):
        for y in range(4):
            for c in range(2):
                dx, dy = (by, 0) if (stage + c) % 2 else (0, by)
                to = ((x + dx) % 4 * 4 + (y + dy) % 4) * 2 + c
                pairs.append(((x * 4 + y) * 2 + c, to))
    return lax.ppermute(value, "seq", pairs)


def swap(value):
    return lax.ppermute(value, "seq", [(q, q ^ 1) for q in range(32)])


def spread(rows, stage):
    return jnp.concatenate([rows] + [turn(rows, stage, k) for k in (1, 2, 3)], axis=0)


def add(parts):
    return sum(p.astype(F32) for p in parts).astype(BF16)


def collect(rows, stage):
    n = rows.shape[0] // 4
    return [rows[:n]] + [turn(rows[k * n : (k + 1) * n], stage, -k) for k in (1, 2, 3)]


def exchange(rows):
    return lax.all_to_all(rows, AXES, split_axis=0, concat_axis=0, tiled=True)


def whole(shape):
    return pl.BlockSpec(shape, lambda j: (0,) * len(shape))


def columns(n, name):
    return pl.BlockSpec((n, BLOCK[name]), lambda j: (0, j))


def slot_columns(name):
    return pl.BlockSpec((DEVICES, CAP, BLOCK[name]), lambda j: (0, 0, j))


def over_columns(name):
    return (D // BLOCK[name],)


def on_device(table, home, item, speeds, forget, gain):
    shape = jax.ShapeDtypeStruct
    slot_rows = shape((DEVICES, CAP, D), BF16)
    wanted, slots = call(
        route_kernel, (shape((DEVICES, 128), I32), shape((1, REQ), I32)), "route"
    )(home.reshape(1, REQ), item.reshape(1, REQ))
    asked = exchange(wanted.reshape(DEVICES, 1, 128)).reshape(DEVICES, 128)
    picked = call(
        pick_kernel,
        slot_rows,
        "pick",
        grid=over_columns("pick"),
        in_specs=[whole((DEVICES, 128)), columns(ITEMS, "pick")],
        out_specs=slot_columns("pick"),
        scratch_shapes=[pltpu.VMEM((ITEMS, SLOTS), BF16)],
    )(asked, table)
    picked, asked, speeds = lax.optimization_barrier((picked, asked, speeds))
    fetched = exchange(picked)
    hot = call(marks_kernel, shape((ITEMS, SLOTS), BF16), "marks", cost=(10**6, 2**20))(asked)
    group = 4
    decay = call(
        decay_kernel,
        shape((HEADS, STEPS, 2 * STEPS), BF16),
        "decay",
        cost=(10**9, 2**23),
        grid=(HEADS // group,),
        in_specs=[
            pl.BlockSpec(memory_space=pltpu.SMEM),
            whole((1, STEPS)),
            whole((STEPS, 1)),
        ],
        out_specs=pl.BlockSpec((group, STEPS, 2 * STEPS), lambda j: (j, 0, 0)),
        scratch_shapes=[pltpu.VMEM((STEPS, STEPS), F32)],
    )(speeds, forget, forget.reshape(STEPS, 1))
    fetched, decay, hot = lax.optimization_barrier((fetched, decay, hot))
    own = call(
        own_negatives_kernel,
        shape((OWN_NEG, D), BF16),
        "own_negatives",
        in_specs=[pl.BlockSpec(memory_space=pltpu.SMEM), pl.BlockSpec(memory_space=pl.ANY)],
        scratch_shapes=[
            pltpu.VMEM((OWN_NEG, CAP, D), BF16),
            pltpu.SemaphoreType.DMA((OWN_NEG,)),
        ],
    )(slots, fetched)
    line = spread(own, 0)
    line, fetched, decay = lax.optimization_barrier((line, fetched, decay))
    near = spread(line, 1)
    x, rep, pos_logit = call(
        state_kernel,
        (shape((STEPS, D), BF16), shape((STEPS, D), BF16), shape((STEPS, 1), F32)),
        "state",
        vmem=40,
        cost=(3 * 10**9, 20 * 2**20),
        grid=over_columns("state"),
        in_specs=[
            whole((1, REQ)),
            slot_columns("state"),
            pl.BlockSpec((BLOCK["state"] // HEAD_DIM, STEPS, 2 * STEPS), lambda j: (j, 0, 0)),
            whole((1, D)),
        ],
        out_specs=(whole((STEPS, D)), whole((STEPS, D)), whole((STEPS, 1))),
        scratch_shapes=[
            pltpu.VMEM((SLOTS, STEPS), BF16),
            pltpu.VMEM((STEPS, D), F32),
            pltpu.VMEM((STEPS, HEAD_DIM), F32),
        ],
    )(slots, fetched, decay, gain.reshape(1, D))
    near, x, rep, pos_logit = lax.optimization_barrier((near, x, rep, pos_logit))
    far = swap(near)
    half_part = shape((NEG // 2, D), BF16)
    loss, d_pos, d_neg, near_part, far_part = call(
        loss_kernel,
        (
            shape((STEPS, 1), F32),
            shape((STEPS, 1), F32),
            shape((STEPS, NEG), BF16),
            half_part,
            half_part,
        ),
        "loss",
        vmem=40,
    )(rep, near, far, pos_logit)
    near_part = add([near_part, swap(far_part)])
    base = call(
        base_kernel,
        slot_rows,
        "base",
        cost=(2 * 10**9, 6 * 2**20),
        grid=over_columns("base"),
        in_specs=[whole((1, REQ)), columns(STEPS, "base"), whole((STEPS, 1))],
        out_specs=slot_columns("base"),
        scratch_shapes=[pltpu.VMEM((SLOTS, STEPS), BF16)],
    )(slots, rep, d_pos)
    line_part = add(collect(near_part, 1))
    base, line_part = lax.optimization_barrier((base, line_part))
    parts = collect(line_part, 0)
    outgoing = call(
        insert_kernel,
        slot_rows,
        "insert",
        in_specs=[pl.BlockSpec(memory_space=pltpu.SMEM), pl.BlockSpec(memory_space=pl.ANY)]
        + [pl.BlockSpec(memory_space=pltpu.VMEM)] * 4,
        out_specs=pl.BlockSpec(memory_space=pl.ANY),
        scratch_shapes=[
            pltpu.VMEM((OWN_NEG, CAP, D), BF16),
            pltpu.SemaphoreType.DMA((OWN_NEG,)),
        ],
        input_output_aliases={1: 0},
    )(slots, base, *parts)
    arrived = exchange(outgoing)
    user_grad = call(
        user_grad_kernel,
        shape((1, STEPS, D), BF16),
        "user_grad",
        cost=(10**9, 6 * 2**20),
        grid=over_columns("user_grad"),
        in_specs=[
            columns(STEPS, "user_grad"),
            whole((STEPS, 1)),
            whole((STEPS, NEG)),
            columns(NEG // 2, "user_grad"),
            columns(NEG // 2, "user_grad"),
        ],
        out_specs=pl.BlockSpec((1, STEPS, BLOCK["user_grad"]), lambda j: (0, 0, j)),
    )(x, d_pos, d_neg, near, far)
    item_grad = call(
        place_kernel,
        shape((ITEMS, D), F32),
        "place",
        grid=over_columns("place"),
        in_specs=[whole((ITEMS, SLOTS)), slot_columns("place")],
        out_specs=columns(ITEMS, "place"),
    )(hot, arrived)
    return loss.reshape(1, STEPS), user_grad, item_grad


def solution(mesh):
    return jax.shard_map(
        on_device,
        mesh=mesh,
        in_specs=(
            P(AXES, None),
            P("dp", "seq", None, None),
            P("dp", "seq", None, None),
            P(AXES, None),
            P(AXES, None),
            P(),
        ),
        out_specs=(P(AXES, None), P(AXES, None, None), P(AXES, None)),
        check_vma=False,
    )
```

```python
import jax
import jax.numpy as jnp
from jax import lax
from jax.experimental import pallas as pl
from jax.experimental.pallas import tpu as pltpu
from jax.sharding import PartitionSpec as P

D = 4096
HEADS = 32
HEAD_DIM = 128
STEPS = 256
OWN_NEG = 8
REQ = STEPS + OWN_NEG
NEG = 256
ITEMS = 512
DEVICES = 128
CAP = 4
SLOTS = DEVICES * CAP
SIGMA = 4.0 / 64.0
BLOCK = dict(pick=1024, state=2048, base=2048, user_grad=2048, place=512)
F32 = jnp.float32
BF16 = jnp.bfloat16
I32 = jnp.int32
AXES = ("dp", "seq")


def iota(shape, dim):
    return lax.broadcasted_iota(I32, shape, dim)


def call(kernel, out_shape, name, cost=None, vmem=40, **kw):
    if cost is not None:
        flops, size = cost
        kw["cost_estimate"] = pl.CostEstimate(flops=flops, bytes_accessed=size, transcendentals=0)
    params = pltpu.CompilerParams(vmem_limit_bytes=vmem * 2**20)
    return pl.pallas_call(kernel, out_shape=out_shape, name=name, compiler_params=params, **kw)


def matmul(a, b, dims):
    return lax.dot_general(a, b, ((dims[0], dims[1]), ((), ())), preferred_element_type=F32)


def route_kernel(owner_row, item_row, wanted, slots):
    row = owner_row[...]
    same = iota((REQ, REQ), 0) == iota((REQ, REQ), 1)
    col = jnp.sum(jnp.where(same, row.astype(F32), 0.0), axis=1, keepdims=True).astype(I32)

    def key(i):
        return jnp.where(i >= STEPS, i - 2 * STEPS, i)

    earlier = key(iota((REQ, REQ), 0)) < key(iota((REQ, REQ), 1))
    rank = jnp.sum(jnp.where((col == row) & earlier, 1.0, 0.0), axis=0, keepdims=True).astype(I32)
    slots[...] = row * CAP + rank
    item = (item_row[...] + 1).astype(F32)
    here = iota((DEVICES, REQ), 0) == row
    lane = iota((DEVICES, 128), 1)
    out = jnp.full((DEVICES, 128), -1.0, F32)
    for s in range(CAP):
        named = jnp.sum(jnp.where(here & (rank == s), item, 0.0), axis=1, keepdims=True)
        out = jnp.where(lane == s, named - 1.0, out)
    wanted[...] = out.astype(I32)


def onehot_items(asked):
    asked = asked.astype(F32)
    device, slot = iota((DEVICES, SLOTS), 0), iota((DEVICES, SLOTS), 1)
    row = jnp.zeros((DEVICES, SLOTS), F32)
    for s in range(CAP):
        row = row + jnp.where(slot == device * CAP + s, asked[:, s : s + 1], 0.0)
    row = jnp.sum(row, axis=0, keepdims=True)
    return (iota((ITEMS, SLOTS), 0).astype(F32) == row).astype(F32).astype(BF16)


def pick_kernel(asked, table, out):
    hot = onehot_items(asked[...]).astype(F32).T.astype(BF16)
    width = BLOCK["pick"]
    for j in range(0, D, width):
        rows = matmul(hot, table[:, j : j + width], ((1,), (0,)))
        out[:, :, j : j + width] = rows.astype(BF16).reshape(DEVICES, CAP, width)


def marks_kernel(asked, hot):
    hot[...] = onehot_items(asked[...])


def place_kernel(hot, arrived, out, held, sems):
    width = held.shape[2]
    stores = []
    for j in range(D // width):
        part = slice(j * width, (j + 1) * width)
        held[j] = matmul(hot[...], arrived[:, :, part].reshape(SLOTS, width), ((1,), (0,)))
        stores.append(pltpu.make_async_copy(held.at[j], out.at[:, part], sems.at[j]))
        stores[-1].start()
    for store in stores:
        store.wait()


def onehot_slots(slots):
    return (iota((SLOTS, slots.shape[1]), 0) == slots).astype(F32).astype(BF16)


def own_negatives_kernel(slots, rows, out, held, sems):
    copies = []
    for k in range(OWN_NEG):
        owner = slots[0, STEPS + k] // CAP
        copies.append(pltpu.make_async_copy(rows.at[owner], held.at[k], sems.at[k]))
        copies[-1].start()
    total = jnp.zeros(out.shape, F32)
    for k in range(OWN_NEG):
        copies[k].wait()
        rank = slots[0, STEPS + k] % CAP
        tile = jnp.where(iota((CAP, D), 0) == rank, held[k].astype(F32), 0.0)
        row = jnp.sum(tile, axis=0, keepdims=True)
        total = jnp.where(iota(out.shape, 0) == k, row, total)
    out[...] = total.astype(BF16)


def state_kernel(
    slots, rows, speeds, forget_row, forget_col, gain, x_out, rep_out, pos_out, hot, base, prior, total
):
    j, last = pl.program_id(0), pl.num_programs(0) - 1
    width = rows.shape[2]
    heads = width // HEAD_DIM
    step, source = iota((STEPS, STEPS), 0), iota((STEPS, STEPS), 1)

    @pl.when(j == 0)
    def _():
        hot[...] = onehot_slots(slots[:, :STEPS])
        total[...] = jnp.zeros_like(total)
        log_row, log_col = jnp.log(1.0 - forget_row[...]), jnp.log(1.0 - forget_col[...])
        until = jnp.sum(jnp.where(source < step, log_row, 0.0), axis=1, keepdims=True)
        through = jnp.sum(jnp.where(step <= source, log_col, 0.0), axis=0, keepdims=True)
        base[...] = jnp.where(source < step, until - through, -1e30)

    x = matmul(hot[...], rows[...].reshape(SLOTS, width), ((0,), (0,))).astype(BF16)
    x_out[:, pl.ds(pl.multiple_of(j * width, width), width)] = x
    span = (step - 1 - source).astype(F32)
    for k in range(heads):
        full = jnp.exp(base[...] - speeds[0, j * heads + k] * span)
        high = full.astype(BF16)
        low = (full - high.astype(F32)).astype(BF16)
        xk = x[:, k * HEAD_DIM : (k + 1) * HEAD_DIM]
        state = matmul(high, xk, ((1,), (0,))) + matmul(low, xk, ((1,), (0,)))
        total[...] += state * state
        prior[:, pl.ds(pl.multiple_of(j * width + k * HEAD_DIM, HEAD_DIM), HEAD_DIM)] = state

    @pl.when(j == last)
    def _():
        norm = lax.rsqrt(jnp.sum(total[...], axis=1, keepdims=True) * (1.0 / D) + 1e-06)
        pos = jnp.zeros((STEPS, HEAD_DIM), F32)
        for c in range(0, D, HEAD_DIM):
            part = slice(c, c + HEAD_DIM)
            rep = (prior[:, part] * norm * gain[:, part]).astype(BF16)
            rep_out[:, part] = rep
            pos = pos + rep.astype(F32) * x_out[:, part].astype(F32)
        pos_out[...] = SIGMA * jnp.sum(pos, axis=1, keepdims=True)


def logits_kernel(rep, negatives, out):
    out[...] = SIGMA * matmul(rep[...], negatives[...], ((1,), (1,)))


def loss_kernel(rep, near_logit, far, pos_logit, loss, d_pos, d_neg, far_part):
    u = rep[...]
    half = NEG // 2
    logits = [near_logit[...], SIGMA * matmul(u, far[...], ((1,), (1,)))]
    pos = pos_logit[...]
    top = jnp.maximum(jnp.max(jnp.maximum(*logits), axis=1, keepdims=True), pos)
    summed = sum(jnp.sum(jnp.exp(l - top), axis=1, keepdims=True) for l in logits)
    log_total = top + jnp.log(jnp.exp(pos - top) + summed)
    valid = jnp.where(iota((STEPS, 1), 0) > 0, 1.0, 0.0)
    loss[...] = (log_total - pos) * valid
    d_pos[...] = (jnp.exp(pos - log_total) - 1.0) * valid
    shares = [(jnp.exp(l - log_total) * valid).astype(BF16) for l in logits]
    d_neg[:, :half] = shares[0]
    d_neg[:, half:] = shares[1]
    far_part[...] = (SIGMA * matmul(shares[1], u, ((0,), (0,)))).astype(BF16)


def near_part_kernel(d_neg, rep, out):
    out[...] = (SIGMA * matmul(d_neg[:, : NEG // 2], rep[...], ((0,), (0,)))).astype(BF16)


def base_kernel(slots, rep, d_pos, out, hot):
    @pl.when(pl.program_id(0) == 0)
    def _():
        hot[...] = onehot_slots(slots[:, :STEPS])

    grad = (SIGMA * d_pos[...] * rep[...].astype(F32)).astype(BF16)
    out[...] = matmul(hot[...], grad, ((1,), (0,))).astype(BF16).reshape(out.shape)


def insert_kernel(slots, base, *refs):
    *parts, out, held, sems = refs
    owners = [slots[0, STEPS + k] // CAP for k in range(OWN_NEG)]
    reads = [
        pltpu.make_async_copy(base.at[owners[k]], held.at[k], sems.at[k]) for k in range(OWN_NEG)
    ]
    for copy in reads:
        copy.start()
    total = sum(p[...].astype(F32) for p in parts)
    for copy in reads:
        copy.wait()
    firsts = []
    for k in range(OWN_NEG):
        first = jnp.int32(k)
        for j in reversed(range(k)):
            first = jnp.where(owners[j] == owners[k], j, first)
        firsts.append(first)
        rank = slots[0, STEPS + k] % CAP
        tile = jnp.where(iota((CAP, D), 0) == rank, total[k : k + 1], held[first].astype(F32))
        held[first] = tile.astype(BF16)
    writes = [
        pltpu.make_async_copy(held.at[k], out.at[owners[k]], sems.at[k]) for k in range(OWN_NEG)
    ]
    for k, copy in enumerate(writes):
        pl.when(firsts[k] == k)(copy.start)
    for k, copy in enumerate(writes):
        pl.when(firsts[k] == k)(copy.wait)


def user_grad_kernel(x, d_pos, d_neg, near, far, out):
    half = NEG // 2
    from_neg = matmul(d_neg[:, :half], near[...], ((1,), (0,))) + matmul(
        d_neg[:, half:], far[...], ((1,), (0,))
    )
    out[0] = (SIGMA * (d_pos[...] * x[...].astype(F32) + from_neg)).astype(BF16)


def turn(value, stage, by):
    pairs = []
    for x in range(4):
        for y in range(4):
            for c in range(2):
                dx, dy = (by, 0) if (stage + c) % 2 else (0, by)
                to = ((x + dx) % 4 * 4 + (y + dy) % 4) * 2 + c
                pairs.append(((x * 4 + y) * 2 + c, to))
    return lax.ppermute(value, "seq", pairs)


def swap(value):
    return lax.ppermute(value, "seq", [(q, q ^ 1) for q in range(32)])


def spread(rows, stage):
    return jnp.concatenate([rows] + [turn(rows, stage, k) for k in (1, 2, 3)], axis=0)


def add(parts):
    return sum(p.astype(F32) for p in parts).astype(BF16)


def collect(rows, stage):
    n = rows.shape[0] // 4
    return [rows[:n]] + [turn(rows[k * n : (k + 1) * n], stage, -k) for k in (1, 2, 3)]


def exchange(rows):
    return lax.all_to_all(rows, AXES, split_axis=0, concat_axis=0, tiled=True)


def whole(shape):
    return pl.BlockSpec(shape, lambda j: (0,) * len(shape))


def columns(n, name):
    return pl.BlockSpec((n, BLOCK[name]), lambda j: (0, j))


def slot_columns(name):
    return pl.BlockSpec((DEVICES, CAP, BLOCK[name]), lambda j: (0, 0, j))


def over_columns(name):
    return (D // BLOCK[name],)


def on_device(table, home, item, speeds, forget, gain):
    shape = jax.ShapeDtypeStruct
    slot_rows = shape((DEVICES, CAP, D), BF16)
    wanted, slots = call(
        route_kernel, (shape((DEVICES, 128), I32), shape((1, REQ), I32)), "route"
    )(home.reshape(1, REQ), item.reshape(1, REQ))
    asked = exchange(wanted.reshape(DEVICES, 1, 128)).reshape(DEVICES, 128)
    picked = call(
        pick_kernel,
        slot_rows,
        "pick",
    )(asked, table)
    fetched = exchange(picked)
    own = call(
        own_negatives_kernel,
        shape((OWN_NEG, D), BF16),
        "own_negatives",
        in_specs=[pl.BlockSpec(memory_space=pltpu.SMEM), pl.BlockSpec(memory_space=pl.ANY)],
        scratch_shapes=[
            pltpu.VMEM((OWN_NEG, CAP, D), BF16),
            pltpu.SemaphoreType.DMA((OWN_NEG,)),
        ],
    )(slots, fetched)
    line = spread(own, 0)
    line, speeds = lax.optimization_barrier((line, speeds))
    near = spread(line, 1)
    x, rep, pos_logit = call(
        state_kernel,
        (shape((STEPS, D), BF16), shape((STEPS, D), BF16), shape((STEPS, 1), F32)),
        "state",
        cost=(3 * 10**9, 20 * 2**20),
        grid=over_columns("state"),
        in_specs=[
            whole((1, REQ)),
            slot_columns("state"),
            pl.BlockSpec(memory_space=pltpu.SMEM),
            whole((1, STEPS)),
            whole((STEPS, 1)),
            whole((1, D)),
        ],
        out_specs=(whole((STEPS, D)), whole((STEPS, D)), whole((STEPS, 1))),
        scratch_shapes=[
            pltpu.VMEM((SLOTS, STEPS), BF16),
            pltpu.VMEM((STEPS, STEPS), F32),
            pltpu.VMEM((STEPS, D), F32),
            pltpu.VMEM((STEPS, HEAD_DIM), F32),
        ],
    )(slots, fetched, speeds, forget, forget.reshape(STEPS, 1), gain.reshape(1, D))
    near, x, rep, pos_logit = lax.optimization_barrier((near, x, rep, pos_logit))
    far = swap(near)
    near_logit = call(logits_kernel, shape((STEPS, NEG // 2), F32), "near_logits")(rep, near)
    far, near_logit = lax.optimization_barrier((far, near_logit))
    half_part = shape((NEG // 2, D), BF16)
    loss, d_pos, d_neg, far_part = call(
        loss_kernel,
        (
            shape((STEPS, 1), F32),
            shape((STEPS, 1), F32),
            shape((STEPS, NEG), BF16),
            half_part,
        ),
        "loss",
    )(rep, near_logit, far, pos_logit)
    from_core = swap(far_part)
    near_part = call(near_part_kernel, half_part, "near_part")(d_neg, rep)
    from_core, near_part = lax.optimization_barrier((from_core, near_part))
    near_part = add([near_part, from_core])
    base = call(
        base_kernel,
        slot_rows,
        "base",
        vmem=62,
        cost=(2 * 10**9, 6 * 2**20),
        grid=over_columns("base"),
        in_specs=[whole((1, REQ)), columns(STEPS, "base"), whole((STEPS, 1))],
        out_specs=slot_columns("base"),
        scratch_shapes=[pltpu.VMEM((SLOTS, STEPS), BF16)],
    )(slots, rep, d_pos)
    line_part = add(collect(near_part, 1))
    user_grad = call(
        user_grad_kernel,
        shape((1, STEPS, D), BF16),
        "user_grad",
        cost=(10**9, 6 * 2**20),
        grid=over_columns("user_grad"),
        in_specs=[
            columns(STEPS, "user_grad"),
            whole((STEPS, 1)),
            whole((STEPS, NEG)),
            columns(NEG // 2, "user_grad"),
            columns(NEG // 2, "user_grad"),
        ],
        out_specs=pl.BlockSpec((1, STEPS, BLOCK["user_grad"]), lambda j: (0, 0, j)),
    )(x, d_pos, d_neg, near, far)
    asked, d_pos = lax.optimization_barrier((asked, d_pos))
    hot = call(marks_kernel, shape((ITEMS, SLOTS), BF16), "marks", cost=(10**6, 2**20))(asked)
    loss = loss.reshape(1, STEPS)
    base, user_grad, line_part = lax.optimization_barrier((base, user_grad, line_part))
    parts = collect(line_part, 0)
    base, hot, loss = lax.optimization_barrier((base, hot, loss))
    outgoing = call(
        insert_kernel,
        slot_rows,
        "insert",
        vmem=62,
        in_specs=[pl.BlockSpec(memory_space=pltpu.SMEM), pl.BlockSpec(memory_space=pl.ANY)]
        + [pl.BlockSpec(memory_space=pltpu.VMEM)] * 4,
        out_specs=pl.BlockSpec(memory_space=pl.ANY),
        scratch_shapes=[
            pltpu.VMEM((OWN_NEG, CAP, D), BF16),
            pltpu.SemaphoreType.DMA((OWN_NEG,)),
        ],
        input_output_aliases={1: 0},
    )(slots, base, *parts)
    arrived = exchange(outgoing)
    item_grad = call(
        place_kernel,
        shape((ITEMS, D), F32),
        "place",
        in_specs=[pl.BlockSpec(memory_space=pltpu.VMEM)] * 2,
        out_specs=pl.BlockSpec(memory_space=pltpu.HBM),
        scratch_shapes=[
            pltpu.VMEM((D // BLOCK["place"], ITEMS, BLOCK["place"]), F32),
            pltpu.SemaphoreType.DMA((D // BLOCK["place"],)),
        ],
    )(hot, arrived)
    return loss, user_grad, item_grad


def solution(mesh):
    return jax.shard_map(
        on_device,
        mesh=mesh,
        in_specs=(
            P(AXES, None),
            P("dp", "seq", None, None),
            P("dp", "seq", None, None),
            P(AXES, None),
            P(AXES, None),
            P(),
        ),
        out_specs=(P(AXES, None), P(AXES, None, None), P(AXES, None)),
        check_vma=False,
    )
```

```python
import jax
import jax.numpy as jnp
from jax import lax
from jax.experimental import pallas as pl
from jax.experimental.pallas import tpu as pltpu
from jax.sharding import PartitionSpec as P

D = 4096
HEADS = 32
HEAD_DIM = 128
STEPS = 256
OWN_NEG = 8
REQ = STEPS + OWN_NEG
NEG = 256
ITEMS = 512
DEVICES = 128
CAP = 4
SLOTS = DEVICES * CAP
SIGMA = 4.0 / 64.0
BLOCK = dict(pick=1024, state=2048, outgoing=1024, user_grad=2048, place=512)
F32 = jnp.float32
BF16 = jnp.bfloat16
I32 = jnp.int32
AXES = ("dp", "seq")


def iota(shape, dim):
    return lax.broadcasted_iota(I32, shape, dim)


def call(kernel, out_shape, name, cost=None, vmem=40, **kw):
    if cost is not None:
        flops, size = cost
        kw["cost_estimate"] = pl.CostEstimate(flops=flops, bytes_accessed=size, transcendentals=0)
    params = pltpu.CompilerParams(vmem_limit_bytes=vmem * 2**20)
    return pl.pallas_call(kernel, out_shape=out_shape, name=name, compiler_params=params, **kw)


def matmul(a, b, dims):
    return lax.dot_general(a, b, ((dims[0], dims[1]), ((), ())), preferred_element_type=F32)


def route_kernel(owner_row, item_row, wanted, slots):
    row = owner_row[...]
    same = iota((REQ, REQ), 0) == iota((REQ, REQ), 1)
    col = jnp.sum(jnp.where(same, row.astype(F32), 0.0), axis=1, keepdims=True).astype(I32)

    def key(i):
        return jnp.where(i >= STEPS, i - 2 * STEPS, i)

    earlier = key(iota((REQ, REQ), 0)) < key(iota((REQ, REQ), 1))
    rank = jnp.sum(jnp.where((col == row) & earlier, 1.0, 0.0), axis=0, keepdims=True).astype(I32)
    slots[...] = row * CAP + rank
    item = (item_row[...] + 1).astype(F32)
    here = iota((DEVICES, REQ), 0) == row
    lane = iota((DEVICES, 128), 1)
    out = jnp.full((DEVICES, 128), -1.0, F32)
    for s in range(CAP):
        named = jnp.sum(jnp.where(here & (rank == s), item, 0.0), axis=1, keepdims=True)
        out = jnp.where(lane == s, named - 1.0, out)
    wanted[...] = out.astype(I32)


def onehot_items(asked):
    asked = asked.astype(F32)
    device, slot = iota((DEVICES, SLOTS), 0), iota((DEVICES, SLOTS), 1)
    row = jnp.zeros((DEVICES, SLOTS), F32)
    for s in range(CAP):
        row = row + jnp.where(slot == device * CAP + s, asked[:, s : s + 1], 0.0)
    row = jnp.sum(row, axis=0, keepdims=True)
    return (iota((ITEMS, SLOTS), 0).astype(F32) == row).astype(F32).astype(BF16)


def pick_kernel(asked, table, out):
    hot = onehot_items(asked[...]).astype(F32).T.astype(BF16)
    width = BLOCK["pick"]
    for j in range(0, D, width):
        rows = matmul(hot, table[:, j : j + width], ((1,), (0,)))
        out[:, :, j : j + width] = rows.astype(BF16).reshape(DEVICES, CAP, width)


def marks_kernel(asked, hot):
    hot[...] = onehot_items(asked[...])


def place_kernel(hot, arrived, out, held, sems):
    width = held.shape[2]
    stores = []
    for j in range(D // width):
        part = slice(j * width, (j + 1) * width)
        held[j] = matmul(hot[...], arrived[:, :, part].reshape(SLOTS, width), ((1,), (0,)))
        stores.append(pltpu.make_async_copy(held.at[j], out.at[:, part], sems.at[j]))
        stores[-1].start()
    for store in stores:
        store.wait()


def onehot_slots(slots):
    return (iota((SLOTS, slots.shape[1]), 0) == slots).astype(F32).astype(BF16)


def own_negatives_kernel(slots, rows, out, held, sems):
    copies = []
    for k in range(OWN_NEG):
        owner = slots[0, STEPS + k] // CAP
        copies.append(pltpu.make_async_copy(rows.at[owner], held.at[k], sems.at[k]))
        copies[-1].start()
    total = jnp.zeros(out.shape, F32)
    for k in range(OWN_NEG):
        copies[k].wait()
        rank = slots[0, STEPS + k] % CAP
        tile = jnp.where(iota((CAP, D), 0) == rank, held[k].astype(F32), 0.0)
        row = jnp.sum(tile, axis=0, keepdims=True)
        total = jnp.where(iota(out.shape, 0) == k, row, total)
    out[...] = total.astype(BF16)


def state_kernel(
    slots, rows, speeds, forget_row, forget_col, gain, x_out, rep_out, pos_out, hot, base, prior, total
):
    j, last = pl.program_id(0), pl.num_programs(0) - 1
    width = rows.shape[2]
    heads = width // HEAD_DIM
    step, source = iota((STEPS, STEPS), 0), iota((STEPS, STEPS), 1)

    @pl.when(j == 0)
    def _():
        hot[...] = onehot_slots(slots[:, :STEPS])
        total[...] = jnp.zeros_like(total)
        log_row, log_col = jnp.log(1.0 - forget_row[...]), jnp.log(1.0 - forget_col[...])
        until = jnp.sum(jnp.where(source < step, log_row, 0.0), axis=1, keepdims=True)
        through = jnp.sum(jnp.where(step <= source, log_col, 0.0), axis=0, keepdims=True)
        base[...] = jnp.where(source < step, until - through, -1e30)

    x = matmul(hot[...], rows[...].reshape(SLOTS, width), ((0,), (0,))).astype(BF16)
    x_out[:, pl.ds(pl.multiple_of(j * width, width), width)] = x
    span = (step - 1 - source).astype(F32)
    for k in range(heads):
        full = jnp.exp(base[...] - speeds[0, j * heads + k] * span)
        high = full.astype(BF16)
        low = (full - high.astype(F32)).astype(BF16)
        xk = x[:, k * HEAD_DIM : (k + 1) * HEAD_DIM]
        state = matmul(high, xk, ((1,), (0,))) + matmul(low, xk, ((1,), (0,)))
        total[...] += state * state
        prior[:, pl.ds(pl.multiple_of(j * width + k * HEAD_DIM, HEAD_DIM), HEAD_DIM)] = state

    @pl.when(j == last)
    def _():
        norm = lax.rsqrt(jnp.sum(total[...], axis=1, keepdims=True) * (1.0 / D) + 1e-06)
        pos = jnp.zeros((STEPS, HEAD_DIM), F32)
        for c in range(0, D, HEAD_DIM):
            part = slice(c, c + HEAD_DIM)
            rep = (prior[:, part] * norm * gain[:, part]).astype(BF16)
            rep_out[:, part] = rep
            pos = pos + rep.astype(F32) * x_out[:, part].astype(F32)
        pos_out[...] = SIGMA * jnp.sum(pos, axis=1, keepdims=True)


def logits_kernel(rep, negatives, out):
    out[...] = SIGMA * matmul(rep[...], negatives[...], ((1,), (1,)))


def loss_kernel(rep, near_logit, far, pos_logit, loss, d_pos, d_neg, far_part):
    u = rep[...]
    half = NEG // 2
    logits = [near_logit[...], SIGMA * matmul(u, far[...], ((1,), (1,)))]
    pos = pos_logit[...]
    top = jnp.maximum(jnp.max(jnp.maximum(*logits), axis=1, keepdims=True), pos)
    summed = sum(jnp.sum(jnp.exp(l - top), axis=1, keepdims=True) for l in logits)
    log_total = top + jnp.log(jnp.exp(pos - top) + summed)
    valid = jnp.where(iota((STEPS, 1), 0) > 0, 1.0, 0.0)
    loss[...] = (log_total - pos) * valid
    d_pos[...] = (jnp.exp(pos - log_total) - 1.0) * valid
    shares = [(jnp.exp(l - log_total) * valid).astype(BF16) for l in logits]
    d_neg[:, :half] = shares[0]
    d_neg[:, half:] = shares[1]
    far_part[...] = (SIGMA * matmul(shares[1], u, ((0,), (0,)))).astype(BF16)


def near_part_kernel(d_neg, rep, out):
    out[...] = (SIGMA * matmul(d_neg[:, : NEG // 2], rep[...], ((0,), (0,)))).astype(BF16)


def outgoing_kernel(slots, own_slots, rep, d_pos, *refs):
    *parts, out = refs
    hot = onehot_slots(slots[:, :STEPS])
    width = BLOCK["outgoing"]
    for j in range(0, D, width):
        part = slice(j, j + width)
        grad = (SIGMA * d_pos[...] * rep[:, part].astype(F32)).astype(BF16)
        rows = matmul(hot, grad, ((1,), (0,))).astype(BF16)
        out[:, :, part] = rows.reshape(DEVICES, CAP, width)
    total = sum(p[...].astype(F32) for p in parts).astype(BF16).astype(F32)
    for k in range(OWN_NEG):
        owner, rank = own_slots[0, STEPS + k] // CAP, own_slots[0, STEPS + k] % CAP
        tile = jnp.where(iota((CAP, D), 0) == rank, total[k : k + 1], out[owner].astype(F32))
        out[owner] = tile.astype(BF16)


def user_grad_kernel(x, d_pos, d_neg, near, far, out):
    half = NEG // 2
    from_neg = matmul(d_neg[:, :half], near[...], ((1,), (0,))) + matmul(
        d_neg[:, half:], far[...], ((1,), (0,))
    )
    out[0] = (SIGMA * (d_pos[...] * x[...].astype(F32) + from_neg)).astype(BF16)


def turn(value, stage, by):
    pairs = []
    for x in range(4):
        for y in range(4):
            for c in range(2):
                dx, dy = (by, 0) if (stage + c) % 2 else (0, by)
                to = ((x + dx) % 4 * 4 + (y + dy) % 4) * 2 + c
                pairs.append(((x * 4 + y) * 2 + c, to))
    return lax.ppermute(value, "seq", pairs)


def swap(value):
    return lax.ppermute(value, "seq", [(q, q ^ 1) for q in range(32)])


def spread(rows, stage):
    return jnp.concatenate([rows] + [turn(rows, stage, k) for k in (1, 2, 3)], axis=0)


def add(parts):
    return sum(p.astype(F32) for p in parts).astype(BF16)


def collect(rows, stage):
    n = rows.shape[0] // 4
    return [rows[:n]] + [turn(rows[k * n : (k + 1) * n], stage, -k) for k in (1, 2, 3)]


def exchange(rows):
    return lax.all_to_all(rows, AXES, split_axis=0, concat_axis=0, tiled=True)


def whole(shape):
    return pl.BlockSpec(shape, lambda j: (0,) * len(shape))


def columns(n, name):
    return pl.BlockSpec((n, BLOCK[name]), lambda j: (0, j))


def slot_columns(name):
    return pl.BlockSpec((DEVICES, CAP, BLOCK[name]), lambda j: (0, 0, j))


def over_columns(name):
    return (D // BLOCK[name],)


def on_device(table, home, item, speeds, forget, gain):
    shape = jax.ShapeDtypeStruct
    slot_rows = shape((DEVICES, CAP, D), BF16)
    wanted, slots = call(
        route_kernel, (shape((DEVICES, 128), I32), shape((1, REQ), I32)), "route"
    )(home.reshape(1, REQ), item.reshape(1, REQ))
    asked = exchange(wanted.reshape(DEVICES, 1, 128)).reshape(DEVICES, 128)
    picked = call(
        pick_kernel,
        slot_rows,
        "pick",
    )(asked, table)
    fetched = exchange(picked)
    own = call(
        own_negatives_kernel,
        shape((OWN_NEG, D), BF16),
        "own_negatives",
        in_specs=[pl.BlockSpec(memory_space=pltpu.SMEM), pl.BlockSpec(memory_space=pl.ANY)],
        scratch_shapes=[
            pltpu.VMEM((OWN_NEG, CAP, D), BF16),
            pltpu.SemaphoreType.DMA((OWN_NEG,)),
        ],
    )(slots, fetched)
    line = spread(own, 0)
    line, speeds = lax.optimization_barrier((line, speeds))
    near = spread(line, 1)
    x, rep, pos_logit = call(
        state_kernel,
        (shape((STEPS, D), BF16), shape((STEPS, D), BF16), shape((STEPS, 1), F32)),
        "state",
        cost=(3 * 10**9, 20 * 2**20),
        grid=over_columns("state"),
        in_specs=[
            whole((1, REQ)),
            slot_columns("state"),
            pl.BlockSpec(memory_space=pltpu.SMEM),
            whole((1, STEPS)),
            whole((STEPS, 1)),
            whole((1, D)),
        ],
        out_specs=(whole((STEPS, D)), whole((STEPS, D)), whole((STEPS, 1))),
        scratch_shapes=[
            pltpu.VMEM((SLOTS, STEPS), BF16),
            pltpu.VMEM((STEPS, STEPS), F32),
            pltpu.VMEM((STEPS, D), F32),
            pltpu.VMEM((STEPS, HEAD_DIM), F32),
        ],
    )(slots, fetched, speeds, forget, forget.reshape(STEPS, 1), gain.reshape(1, D))
    near, x, rep, pos_logit = lax.optimization_barrier((near, x, rep, pos_logit))
    far = swap(near)
    near_logit = call(logits_kernel, shape((STEPS, NEG // 2), F32), "near_logits")(rep, near)
    far, near_logit = lax.optimization_barrier((far, near_logit))
    half_part = shape((NEG // 2, D), BF16)
    loss, d_pos, d_neg, far_part = call(
        loss_kernel,
        (
            shape((STEPS, 1), F32),
            shape((STEPS, 1), F32),
            shape((STEPS, NEG), BF16),
            half_part,
        ),
        "loss",
    )(rep, near_logit, far, pos_logit)
    from_core = swap(far_part)
    near_part = call(near_part_kernel, half_part, "near_part")(d_neg, rep)
    from_core, near_part = lax.optimization_barrier((from_core, near_part))
    near_part = add([near_part, from_core])
    line_part = add(collect(near_part, 1))
    user_grad = call(
        user_grad_kernel,
        shape((1, STEPS, D), BF16),
        "user_grad",
        cost=(10**9, 6 * 2**20),
        grid=over_columns("user_grad"),
        in_specs=[
            columns(STEPS, "user_grad"),
            whole((STEPS, 1)),
            whole((STEPS, NEG)),
            columns(NEG // 2, "user_grad"),
            columns(NEG // 2, "user_grad"),
        ],
        out_specs=pl.BlockSpec((1, STEPS, BLOCK["user_grad"]), lambda j: (0, 0, j)),
    )(x, d_pos, d_neg, near, far)
    asked, d_pos = lax.optimization_barrier((asked, d_pos))
    hot = call(marks_kernel, shape((ITEMS, SLOTS), BF16), "marks", cost=(10**6, 2**20))(asked)
    loss = loss.reshape(1, STEPS)
    user_grad, line_part = lax.optimization_barrier((user_grad, line_part))
    parts = collect(line_part, 0)
    parts, hot, loss = lax.optimization_barrier((parts, hot, loss))
    outgoing = call(
        outgoing_kernel,
        slot_rows,
        "outgoing",
        in_specs=[pl.BlockSpec(memory_space=pltpu.VMEM), pl.BlockSpec(memory_space=pltpu.SMEM)]
        + [pl.BlockSpec(memory_space=pltpu.VMEM)] * 6,
    )(slots, slots, rep, d_pos, *parts)
    arrived = exchange(outgoing)
    item_grad = call(
        place_kernel,
        shape((ITEMS, D), F32),
        "place",
        in_specs=[pl.BlockSpec(memory_space=pltpu.VMEM)] * 2,
        out_specs=pl.BlockSpec(memory_space=pltpu.HBM),
        scratch_shapes=[
            pltpu.VMEM((D // BLOCK["place"], ITEMS, BLOCK["place"]), F32),
            pltpu.SemaphoreType.DMA((D // BLOCK["place"],)),
        ],
    )(hot, arrived)
    return loss, user_grad, item_grad


def solution(mesh):
    return jax.shard_map(
        on_device,
        mesh=mesh,
        in_specs=(
            P(AXES, None),
            P("dp", "seq", None, None),
            P("dp", "seq", None, None),
            P(AXES, None),
            P(AXES, None),
            P(),
        ),
        out_specs=(P(AXES, None), P(AXES, None, None), P(AXES, None)),
        check_vma=False,
    )
```

```python
import jax
import jax.numpy as jnp
from jax import lax
from jax.experimental import pallas as pl
from jax.experimental.pallas import tpu as pltpu
from jax.sharding import PartitionSpec as P

D = 4096
HEADS = 32
HEAD_DIM = 128
STEPS = 256
OWN_NEG = 8
REQ = STEPS + OWN_NEG
NEG = 256
ITEMS = 512
DEVICES = 128
CAP = 4
SLOTS = DEVICES * CAP
SIGMA = 4.0 / 64.0
BLOCK = dict(pick=1024, state=2048, outgoing=1024, user_grad=2048, place=512)
F32 = jnp.float32
BF16 = jnp.bfloat16
I32 = jnp.int32
AXES = ("dp", "seq")


def iota(shape, dim):
    return lax.broadcasted_iota(I32, shape, dim)


def call(kernel, out_shape, name, cost=None, vmem=40, **kw):
    if cost is not None:
        flops, size = cost
        kw["cost_estimate"] = pl.CostEstimate(flops=flops, bytes_accessed=size, transcendentals=0)
    params = pltpu.CompilerParams(vmem_limit_bytes=vmem * 2**20)
    return pl.pallas_call(kernel, out_shape=out_shape, name=name, compiler_params=params, **kw)


def matmul(a, b, dims):
    return lax.dot_general(a, b, ((dims[0], dims[1]), ((), ())), preferred_element_type=F32)


def route_kernel(home, names, table, wanted, slots, near_table, owner_row, item_row, sems):
    first = pltpu.make_async_copy(home, owner_row, sems.at[0])
    second = pltpu.make_async_copy(names, item_row, sems.at[1])
    move = pltpu.make_async_copy(table, near_table, sems.at[2])
    first.start()
    second.start()
    move.start()
    first.wait()
    second.wait()
    row = owner_row[...]
    same = iota((REQ, REQ), 0) == iota((REQ, REQ), 1)
    col = jnp.sum(jnp.where(same, row.astype(F32), 0.0), axis=1, keepdims=True).astype(I32)

    def key(i):
        return jnp.where(i >= STEPS, i - 2 * STEPS, i)

    earlier = key(iota((REQ, REQ), 0)) < key(iota((REQ, REQ), 1))
    rank = jnp.sum(jnp.where((col == row) & earlier, 1.0, 0.0), axis=0, keepdims=True).astype(I32)
    slots[...] = row * CAP + rank
    item = (item_row[...] + 1).astype(F32)
    here = iota((DEVICES, REQ), 0) == row
    lane = iota((DEVICES, 128), 1)
    out = jnp.full((DEVICES, 128), -1.0, F32)
    for s in range(CAP):
        named = jnp.sum(jnp.where(here & (rank == s), item, 0.0), axis=1, keepdims=True)
        out = jnp.where(lane == s, named - 1.0, out)
    wanted[...] = out.astype(I32)
    move.wait()


def onehot_items(asked):
    asked = asked.astype(F32)
    device, slot = iota((DEVICES, SLOTS), 0), iota((DEVICES, SLOTS), 1)
    row = jnp.zeros((DEVICES, SLOTS), F32)
    for s in range(CAP):
        row = row + jnp.where(slot == device * CAP + s, asked[:, s : s + 1], 0.0)
    row = jnp.sum(row, axis=0, keepdims=True)
    return (iota((ITEMS, SLOTS), 0).astype(F32) == row).astype(F32).astype(BF16)


def pick_kernel(asked, table, out):
    hot = onehot_items(asked[...]).astype(F32).T.astype(BF16)
    width = BLOCK["pick"]
    for j in range(0, D, width):
        rows = matmul(hot, table[:, j : j + width], ((1,), (0,)))
        out[:, :, j : j + width] = rows.astype(BF16).reshape(DEVICES, CAP, width)


def marks_kernel(asked, hot):
    hot[...] = onehot_items(asked[...])


def place_kernel(hot, arrived, out, held, sems):
    width = held.shape[2]
    stores = []
    for j in range(D // width):
        part = slice(j * width, (j + 1) * width)
        held[j] = matmul(hot[...], arrived[:, :, part].reshape(SLOTS, width), ((1,), (0,)))
        stores.append(pltpu.make_async_copy(held.at[j], out.at[:, part], sems.at[j]))
        stores[-1].start()
    for store in stores:
        store.wait()


def onehot_slots(slots):
    return (iota((SLOTS, slots.shape[1]), 0) == slots).astype(F32).astype(BF16)


def own_negatives_kernel(slots, rows, out, held, sems):
    copies = []
    for k in range(OWN_NEG):
        owner = slots[0, STEPS + k] // CAP
        copies.append(pltpu.make_async_copy(rows.at[owner], held.at[k], sems.at[k]))
        copies[-1].start()
    total = jnp.zeros(out.shape, F32)
    for k in range(OWN_NEG):
        copies[k].wait()
        rank = slots[0, STEPS + k] % CAP
        tile = jnp.where(iota((CAP, D), 0) == rank, held[k].astype(F32), 0.0)
        row = jnp.sum(tile, axis=0, keepdims=True)
        total = jnp.where(iota(out.shape, 0) == k, row, total)
    out[...] = total.astype(BF16)


def state_kernel(
    slots, rows, speeds, forget_row, forget_col, gain, x_out, rep_out, pos_out, hot, base, prior, total
):
    j, last = pl.program_id(0), pl.num_programs(0) - 1
    width = rows.shape[2]
    heads = width // HEAD_DIM
    step, source = iota((STEPS, STEPS), 0), iota((STEPS, STEPS), 1)

    @pl.when(j == 0)
    def _():
        hot[...] = onehot_slots(slots[:, :STEPS])
        total[...] = jnp.zeros_like(total)
        log_row, log_col = jnp.log(1.0 - forget_row[...]), jnp.log(1.0 - forget_col[...])
        until = jnp.sum(jnp.where(source < step, log_row, 0.0), axis=1, keepdims=True)
        through = jnp.sum(jnp.where(step <= source, log_col, 0.0), axis=0, keepdims=True)
        base[...] = jnp.where(source < step, until - through, -1e30)

    x = matmul(hot[...], rows[...].reshape(SLOTS, width), ((0,), (0,))).astype(BF16)
    x_out[:, pl.ds(pl.multiple_of(j * width, width), width)] = x
    span = (step - 1 - source).astype(F32)
    for k in range(heads):
        full = jnp.exp(base[...] - speeds[0, j * heads + k] * span)
        high = full.astype(BF16)
        low = (full - high.astype(F32)).astype(BF16)
        xk = x[:, k * HEAD_DIM : (k + 1) * HEAD_DIM]
        state = matmul(high, xk, ((1,), (0,))) + matmul(low, xk, ((1,), (0,)))
        total[...] += state * state
        prior[:, pl.ds(pl.multiple_of(j * width + k * HEAD_DIM, HEAD_DIM), HEAD_DIM)] = state

    @pl.when(j == last)
    def _():
        norm = lax.rsqrt(jnp.sum(total[...], axis=1, keepdims=True) * (1.0 / D) + 1e-06)
        pos = jnp.zeros((STEPS, HEAD_DIM), F32)
        for c in range(0, D, HEAD_DIM):
            part = slice(c, c + HEAD_DIM)
            rep = (prior[:, part] * norm * gain[:, part]).astype(BF16)
            rep_out[:, part] = rep
            pos = pos + rep.astype(F32) * x_out[:, part].astype(F32)
        pos_out[...] = SIGMA * jnp.sum(pos, axis=1, keepdims=True)


def logits_kernel(rep, negatives, out):
    out[...] = SIGMA * matmul(rep[...], negatives[...], ((1,), (1,)))


def loss_kernel(rep, near_logit, far, pos_logit, loss, d_pos, d_neg, far_part):
    u = rep[...]
    half = NEG // 2
    logits = [near_logit[...], SIGMA * matmul(u, far[...], ((1,), (1,)))]
    pos = pos_logit[...]
    top = jnp.maximum(jnp.max(jnp.maximum(*logits), axis=1, keepdims=True), pos)
    summed = sum(jnp.sum(jnp.exp(l - top), axis=1, keepdims=True) for l in logits)
    log_total = top + jnp.log(jnp.exp(pos - top) + summed)
    valid = jnp.where(iota((STEPS, 1), 0) > 0, 1.0, 0.0)
    loss[...] = (log_total - pos) * valid
    d_pos[...] = (jnp.exp(pos - log_total) - 1.0) * valid
    shares = [(jnp.exp(l - log_total) * valid).astype(BF16) for l in logits]
    d_neg[:, :half] = shares[0]
    d_neg[:, half:] = shares[1]
    far_part[...] = (SIGMA * matmul(shares[1], u, ((0,), (0,)))).astype(BF16)


def near_part_kernel(d_neg, rep, out):
    out[...] = (SIGMA * matmul(d_neg[:, : NEG // 2], rep[...], ((0,), (0,)))).astype(BF16)


def outgoing_kernel(slots, own_slots, rep, d_pos, *refs):
    *parts, out = refs
    hot = onehot_slots(slots[:, :STEPS])
    width = BLOCK["outgoing"]
    for j in range(0, D, width):
        part = slice(j, j + width)
        grad = (SIGMA * d_pos[...] * rep[:, part].astype(F32)).astype(BF16)
        rows = matmul(hot, grad, ((1,), (0,))).astype(BF16)
        out[:, :, part] = rows.reshape(DEVICES, CAP, width)
    total = sum(p[...].astype(F32) for p in parts).astype(BF16).astype(F32)
    for k in range(OWN_NEG):
        owner, rank = own_slots[0, STEPS + k] // CAP, own_slots[0, STEPS + k] % CAP
        tile = jnp.where(iota((CAP, D), 0) == rank, total[k : k + 1], out[owner].astype(F32))
        out[owner] = tile.astype(BF16)


def user_grad_kernel(x, d_pos, d_neg, near, far, out):
    half = NEG // 2
    from_neg = matmul(d_neg[:, :half], near[...], ((1,), (0,))) + matmul(
        d_neg[:, half:], far[...], ((1,), (0,))
    )
    out[0] = (SIGMA * (d_pos[...] * x[...].astype(F32) + from_neg)).astype(BF16)


def turn(value, stage, by):
    pairs = []
    for x in range(4):
        for y in range(4):
            for c in range(2):
                dx, dy = (by, 0) if (stage + c) % 2 else (0, by)
                to = ((x + dx) % 4 * 4 + (y + dy) % 4) * 2 + c
                pairs.append(((x * 4 + y) * 2 + c, to))
    return lax.ppermute(value, "seq", pairs)


def swap(value):
    return lax.ppermute(value, "seq", [(q, q ^ 1) for q in range(32)])


def spread(rows, stage):
    return jnp.concatenate([rows] + [turn(rows, stage, k) for k in (1, 2, 3)], axis=0)


def add(parts):
    return sum(p.astype(F32) for p in parts).astype(BF16)


def collect(rows, stage):
    n = rows.shape[0] // 4
    return [rows[:n]] + [turn(rows[k * n : (k + 1) * n], stage, -k) for k in (1, 2, 3)]


def exchange(rows):
    return lax.all_to_all(rows, AXES, split_axis=0, concat_axis=0, tiled=True)


def whole(shape):
    return pl.BlockSpec(shape, lambda j: (0,) * len(shape))


def columns(n, name):
    return pl.BlockSpec((n, BLOCK[name]), lambda j: (0, j))


def slot_columns(name):
    return pl.BlockSpec((DEVICES, CAP, BLOCK[name]), lambda j: (0, 0, j))


def over_columns(name):
    return (D // BLOCK[name],)


def on_device(table, home, item, speeds, forget, gain):
    shape = jax.ShapeDtypeStruct
    slot_rows = shape((DEVICES, CAP, D), BF16)
    in_hbm = lambda a: pltpu.with_memory_space_constraint(a, pltpu.HBM)
    wanted, slots, near_table = call(
        route_kernel,
        (shape((DEVICES, 128), I32), shape((1, REQ), I32), pltpu.VMEM((ITEMS, D), BF16)),
        "route",
        vmem=16,
        in_specs=[pl.BlockSpec(memory_space=pltpu.HBM)] * 3,
        out_specs=(
            pl.BlockSpec(memory_space=pltpu.VMEM),
            pl.BlockSpec(memory_space=pltpu.VMEM),
            pl.BlockSpec(memory_space=pltpu.VMEM),
        ),
        scratch_shapes=[
            pltpu.VMEM((1, REQ), I32),
            pltpu.VMEM((1, REQ), I32),
            pltpu.SemaphoreType.DMA((3,)),
        ],
    )(in_hbm(home.reshape(1, REQ)), in_hbm(item.reshape(1, REQ)), in_hbm(table))
    asked = exchange(wanted.reshape(DEVICES, 1, 128)).reshape(DEVICES, 128)
    picked = call(
        pick_kernel,
        slot_rows,
        "pick",
    )(asked, near_table)
    fetched = exchange(picked)
    own = call(
        own_negatives_kernel,
        shape((OWN_NEG, D), BF16),
        "own_negatives",
        in_specs=[pl.BlockSpec(memory_space=pltpu.SMEM), pl.BlockSpec(memory_space=pl.ANY)],
        scratch_shapes=[
            pltpu.VMEM((OWN_NEG, CAP, D), BF16),
            pltpu.SemaphoreType.DMA((OWN_NEG,)),
        ],
    )(slots, fetched)
    line = spread(own, 0)
    line, speeds = lax.optimization_barrier((line, speeds))
    near = spread(line, 1)
    x, rep, pos_logit = call(
        state_kernel,
        (shape((STEPS, D), BF16), shape((STEPS, D), BF16), shape((STEPS, 1), F32)),
        "state",
        cost=(3 * 10**9, 20 * 2**20),
        grid=over_columns("state"),
        in_specs=[
            whole((1, REQ)),
            slot_columns("state"),
            pl.BlockSpec(memory_space=pltpu.SMEM),
            whole((1, STEPS)),
            whole((STEPS, 1)),
            whole((1, D)),
        ],
        out_specs=(whole((STEPS, D)), whole((STEPS, D)), whole((STEPS, 1))),
        scratch_shapes=[
            pltpu.VMEM((SLOTS, STEPS), BF16),
            pltpu.VMEM((STEPS, STEPS), F32),
            pltpu.VMEM((STEPS, D), F32),
            pltpu.VMEM((STEPS, HEAD_DIM), F32),
        ],
    )(slots, fetched, speeds, forget, forget.reshape(STEPS, 1), gain.reshape(1, D))
    near, x, rep, pos_logit = lax.optimization_barrier((near, x, rep, pos_logit))
    far = swap(near)
    near_logit = call(logits_kernel, shape((STEPS, NEG // 2), F32), "near_logits")(rep, near)
    far, near_logit = lax.optimization_barrier((far, near_logit))
    half_part = shape((NEG // 2, D), BF16)
    loss, d_pos, d_neg, far_part = call(
        loss_kernel,
        (
            shape((STEPS, 1), F32),
            shape((STEPS, 1), F32),
            shape((STEPS, NEG), BF16),
            half_part,
        ),
        "loss",
    )(rep, near_logit, far, pos_logit)
    from_core = swap(far_part)
    near_part = call(near_part_kernel, half_part, "near_part")(d_neg, rep)
    from_core, near_part = lax.optimization_barrier((from_core, near_part))
    near_part = add([near_part, from_core])
    line_part = add(collect(near_part, 1))
    user_grad = call(
        user_grad_kernel,
        shape((1, STEPS, D), BF16),
        "user_grad",
        cost=(10**9, 6 * 2**20),
        grid=over_columns("user_grad"),
        in_specs=[
            columns(STEPS, "user_grad"),
            whole((STEPS, 1)),
            whole((STEPS, NEG)),
            columns(NEG // 2, "user_grad"),
            columns(NEG // 2, "user_grad"),
        ],
        out_specs=pl.BlockSpec((1, STEPS, BLOCK["user_grad"]), lambda j: (0, 0, j)),
    )(x, d_pos, d_neg, near, far)
    asked, d_pos = lax.optimization_barrier((asked, d_pos))
    hot = call(marks_kernel, shape((ITEMS, SLOTS), BF16), "marks", cost=(10**6, 2**20))(asked)
    loss = loss.reshape(1, STEPS)
    user_grad, line_part = lax.optimization_barrier((user_grad, line_part))
    parts = collect(line_part, 0)
    parts, hot, loss = lax.optimization_barrier((parts, hot, loss))
    outgoing = call(
        outgoing_kernel,
        slot_rows,
        "outgoing",
        in_specs=[pl.BlockSpec(memory_space=pltpu.VMEM), pl.BlockSpec(memory_space=pltpu.SMEM)]
        + [pl.BlockSpec(memory_space=pltpu.VMEM)] * 6,
    )(slots, slots, rep, d_pos, *parts)
    arrived = exchange(outgoing)
    item_grad = call(
        place_kernel,
        shape((ITEMS, D), F32),
        "place",
        in_specs=[pl.BlockSpec(memory_space=pltpu.VMEM)] * 2,
        out_specs=pl.BlockSpec(memory_space=pltpu.HBM),
        scratch_shapes=[
            pltpu.VMEM((D // BLOCK["place"], ITEMS, BLOCK["place"]), F32),
            pltpu.SemaphoreType.DMA((D // BLOCK["place"],)),
        ],
    )(hot, arrived)
    return loss, user_grad, item_grad


def solution(mesh):
    return jax.shard_map(
        on_device,
        mesh=mesh,
        in_specs=(
            P(AXES, None),
            P("dp", "seq", None, None),
            P("dp", "seq", None, None),
            P(AXES, None),
            P(AXES, None),
            P(),
        ),
        out_specs=(P(AXES, None), P(AXES, None, None), P(AXES, None)),
        check_vma=False,
    )
```

```python
import jax
import jax.numpy as jnp
from jax import lax
from jax.experimental import pallas as pl
from jax.experimental.pallas import tpu as pltpu
from jax.sharding import PartitionSpec as P

D = 4096
HEADS = 32
HEAD_DIM = 128
STEPS = 256
OWN_NEG = 8
REQ = STEPS + OWN_NEG
NEG = 256
ORDER = ((1, 2, 3), (2, 1, 3))
ITEMS = 512
DEVICES = 128
CAP = 4
SLOTS = DEVICES * CAP
SIGMA = 4.0 / 64.0
BLOCK = dict(pick=1024, state=2048, outgoing=1024, user_grad=2048, place=512)
F32 = jnp.float32
BF16 = jnp.bfloat16
I32 = jnp.int32
AXES = ("dp", "seq")


def iota(shape, dim):
    return lax.broadcasted_iota(I32, shape, dim)


def call(kernel, out_shape, name, cost=None, vmem=40, **kw):
    if cost is not None:
        flops, size = cost
        kw["cost_estimate"] = pl.CostEstimate(flops=flops, bytes_accessed=size, transcendentals=0)
    params = pltpu.CompilerParams(vmem_limit_bytes=vmem * 2**20)
    return pl.pallas_call(kernel, out_shape=out_shape, name=name, compiler_params=params, **kw)


def matmul(a, b, dims):
    return lax.dot_general(a, b, ((dims[0], dims[1]), ((), ())), preferred_element_type=F32)


def route_kernel(home, names, table, wanted, slots, near_table, owner_row, item_row, sems):
    first = pltpu.make_async_copy(home, owner_row, sems.at[0])
    second = pltpu.make_async_copy(names, item_row, sems.at[1])
    move = pltpu.make_async_copy(table, near_table, sems.at[2])
    first.start()
    second.start()
    move.start()
    first.wait()
    second.wait()
    row = owner_row[...]
    same = iota((REQ, REQ), 0) == iota((REQ, REQ), 1)
    col = jnp.sum(jnp.where(same, row.astype(F32), 0.0), axis=1, keepdims=True).astype(I32)

    def key(i):
        return jnp.where(i >= STEPS, i - 2 * STEPS, i)

    earlier = key(iota((REQ, REQ), 0)) < key(iota((REQ, REQ), 1))
    rank = jnp.sum(jnp.where((col == row) & earlier, 1.0, 0.0), axis=0, keepdims=True).astype(I32)
    slots[...] = row * CAP + rank
    item = (item_row[...] + 1).astype(F32)
    here = iota((DEVICES, REQ), 0) == row
    lane = iota((DEVICES, 128), 1)
    out = jnp.full((DEVICES, 128), -1.0, F32)
    for s in range(CAP):
        named = jnp.sum(jnp.where(here & (rank == s), item, 0.0), axis=1, keepdims=True)
        out = jnp.where(lane == s, named - 1.0, out)
    wanted[...] = out.astype(I32)
    move.wait()


def onehot_items(asked):
    asked = asked.astype(F32)
    device, slot = iota((DEVICES, SLOTS), 0), iota((DEVICES, SLOTS), 1)
    row = jnp.zeros((DEVICES, SLOTS), F32)
    for s in range(CAP):
        row = row + jnp.where(slot == device * CAP + s, asked[:, s : s + 1], 0.0)
    row = jnp.sum(row, axis=0, keepdims=True)
    return (iota((ITEMS, SLOTS), 0).astype(F32) == row).astype(F32).astype(BF16)


def pick_kernel(asked, table, out):
    hot = onehot_items(asked[...]).astype(F32).T.astype(BF16)
    width = BLOCK["pick"]
    for j in range(0, D, width):
        rows = matmul(hot, table[:, j : j + width], ((1,), (0,)))
        out[:, :, j : j + width] = rows.astype(BF16).reshape(DEVICES, CAP, width)


def marks_kernel(asked, hot):
    hot[...] = onehot_items(asked[...])


def place_kernel(hot, arrived, out, held, sems):
    width = held.shape[2]
    stores = []
    for j in range(D // width):
        part = slice(j * width, (j + 1) * width)
        held[j] = matmul(hot[...], arrived[:, :, part].reshape(SLOTS, width), ((1,), (0,)))
        stores.append(pltpu.make_async_copy(held.at[j], out.at[:, part], sems.at[j]))
        stores[-1].start()
    for store in stores:
        store.wait()


def onehot_slots(slots):
    return (iota((SLOTS, slots.shape[1]), 0) == slots).astype(F32).astype(BF16)


def own_negatives_kernel(slots, rows, out, held, sems):
    copies = []
    for k in range(OWN_NEG):
        owner = slots[0, STEPS + k] // CAP
        copies.append(pltpu.make_async_copy(rows.at[owner], held.at[k], sems.at[k]))
        copies[-1].start()
    total = jnp.zeros(out.shape, F32)
    for k in range(OWN_NEG):
        copies[k].wait()
        rank = slots[0, STEPS + k] % CAP
        tile = jnp.where(iota((CAP, D), 0) == rank, held[k].astype(F32), 0.0)
        row = jnp.sum(tile, axis=0, keepdims=True)
        total = jnp.where(iota(out.shape, 0) == k, row, total)
    out[...] = total.astype(BF16)


def state_kernel(
    slots, rows, speeds, forget_row, forget_col, gain, x_out, rep_out, pos_out, hot, base, prior, total
):
    j, last = pl.program_id(0), pl.num_programs(0) - 1
    width = rows.shape[2]
    heads = width // HEAD_DIM
    step, source = iota((STEPS, STEPS), 0), iota((STEPS, STEPS), 1)

    @pl.when(j == 0)
    def _():
        hot[...] = onehot_slots(slots[:, :STEPS])
        total[...] = jnp.zeros_like(total)
        log_row, log_col = jnp.log(1.0 - forget_row[...]), jnp.log(1.0 - forget_col[...])
        until = jnp.sum(jnp.where(source < step, log_row, 0.0), axis=1, keepdims=True)
        through = jnp.sum(jnp.where(step <= source, log_col, 0.0), axis=0, keepdims=True)
        base[...] = jnp.where(source < step, until - through, -1e30)

    x = matmul(hot[...], rows[...].reshape(SLOTS, width), ((0,), (0,))).astype(BF16)
    x_out[:, pl.ds(pl.multiple_of(j * width, width), width)] = x
    span = (step - 1 - source).astype(F32)
    for k in range(heads):
        full = jnp.exp(base[...] - speeds[0, j * heads + k] * span)
        high = full.astype(BF16)
        low = (full - high.astype(F32)).astype(BF16)
        xk = x[:, k * HEAD_DIM : (k + 1) * HEAD_DIM]
        state = matmul(high, xk, ((1,), (0,))) + matmul(low, xk, ((1,), (0,)))
        total[...] += state * state
        prior[:, pl.ds(pl.multiple_of(j * width + k * HEAD_DIM, HEAD_DIM), HEAD_DIM)] = state

    @pl.when(j == last)
    def _():
        norm = lax.rsqrt(jnp.sum(total[...], axis=1, keepdims=True) * (1.0 / D) + 1e-06)
        pos = jnp.zeros((STEPS, HEAD_DIM), F32)
        for c in range(0, D, HEAD_DIM):
            part = slice(c, c + HEAD_DIM)
            rep = (prior[:, part] * norm * gain[:, part]).astype(BF16)
            rep_out[:, part] = rep
            pos = pos + rep.astype(F32) * x_out[:, part].astype(F32)
        pos_out[...] = SIGMA * jnp.sum(pos, axis=1, keepdims=True)


def logits_kernel(rep, negatives, out):
    out[...] = SIGMA * matmul(rep[...], negatives[...], ((1,), (1,)))


def loss_kernel(rep, near_logit, far, pos_logit, loss, d_pos, d_neg, far_part):
    u = rep[...]
    half = NEG // 2
    logits = [near_logit[...], SIGMA * matmul(u, far[...], ((1,), (1,)))]
    pos = pos_logit[...]
    top = jnp.maximum(jnp.max(jnp.maximum(*logits), axis=1, keepdims=True), pos)
    summed = sum(jnp.sum(jnp.exp(l - top), axis=1, keepdims=True) for l in logits)
    log_total = top + jnp.log(jnp.exp(pos - top) + summed)
    valid = jnp.where(iota((STEPS, 1), 0) > 0, 1.0, 0.0)
    loss[...] = (log_total - pos) * valid
    d_pos[...] = (jnp.exp(pos - log_total) - 1.0) * valid
    shares = [(jnp.exp(l - log_total) * valid).astype(BF16) for l in logits]
    d_neg[:, :half] = shares[0]
    d_neg[:, half:] = shares[1]
    far_part[...] = (SIGMA * matmul(shares[1], u, ((0,), (0,)))).astype(BF16)


def near_part_kernel(d_neg, rep, out):
    out[...] = (SIGMA * matmul(d_neg[:, : NEG // 2], rep[...], ((0,), (0,)))).astype(BF16)


def outgoing_kernel(slots, own_slots, rep, d_pos, *refs):
    *parts, out = refs
    hot = onehot_slots(slots[:, :STEPS])
    width = BLOCK["outgoing"]
    for j in range(0, D, width):
        part = slice(j, j + width)
        grad = (SIGMA * d_pos[...] * rep[:, part].astype(F32)).astype(BF16)
        rows = matmul(hot, grad, ((1,), (0,))).astype(BF16)
        out[:, :, part] = rows.reshape(DEVICES, CAP, width)
    total = sum(p[...].astype(F32) for p in parts).astype(BF16).astype(F32)
    for k in range(OWN_NEG):
        owner, rank = own_slots[0, STEPS + k] // CAP, own_slots[0, STEPS + k] % CAP
        tile = jnp.where(iota((CAP, D), 0) == rank, total[k : k + 1], out[owner].astype(F32))
        out[owner] = tile.astype(BF16)


def user_grad_kernel(x, d_pos, d_neg, near, far, out):
    half = NEG // 2
    from_neg = matmul(d_neg[:, :half], near[...], ((1,), (0,))) + matmul(
        d_neg[:, half:], far[...], ((1,), (0,))
    )
    out[0] = (SIGMA * (d_pos[...] * x[...].astype(F32) + from_neg)).astype(BF16)


def turn(value, stage, by):
    pairs = []
    for x in range(4):
        for y in range(4):
            for c in range(2):
                dx, dy = (by, 0) if (stage + c) % 2 else (0, by)
                to = ((x + dx) % 4 * 4 + (y + dy) % 4) * 2 + c
                pairs.append(((x * 4 + y) * 2 + c, to))
    return lax.ppermute(value, "seq", pairs)


def swap(value):
    return lax.ppermute(value, "seq", [(q, q ^ 1) for q in range(32)])


def spread(rows, stage):
    return jnp.concatenate([rows] + [turn(rows, stage, k) for k in ORDER[stage]], axis=0)


def add(parts):
    return sum(p.astype(F32) for p in parts).astype(BF16)


def collect(rows, stage):
    n = rows.shape[0] // 4
    return [rows[:n]] + [
        turn(rows[k * n : (k + 1) * n], stage, -by) for k, by in enumerate(ORDER[stage], 1)
    ]


def exchange(rows):
    return lax.all_to_all(rows, AXES, split_axis=0, concat_axis=0, tiled=True)


def whole(shape):
    return pl.BlockSpec(shape, lambda j: (0,) * len(shape))


def columns(n, name):
    return pl.BlockSpec((n, BLOCK[name]), lambda j: (0, j))


def slot_columns(name):
    return pl.BlockSpec((DEVICES, CAP, BLOCK[name]), lambda j: (0, 0, j))


def over_columns(name):
    return (D // BLOCK[name],)


def on_device(table, home, item, speeds, forget, gain):
    shape = jax.ShapeDtypeStruct
    slot_rows = shape((DEVICES, CAP, D), BF16)
    in_hbm = lambda a: pltpu.with_memory_space_constraint(a, pltpu.HBM)
    wanted, slots, near_table = call(
        route_kernel,
        (shape((DEVICES, 128), I32), shape((1, REQ), I32), pltpu.VMEM((ITEMS, D), BF16)),
        "route",
        vmem=16,
        in_specs=[pl.BlockSpec(memory_space=pltpu.HBM)] * 3,
        out_specs=(
            pl.BlockSpec(memory_space=pltpu.VMEM),
            pl.BlockSpec(memory_space=pltpu.VMEM),
            pl.BlockSpec(memory_space=pltpu.VMEM),
        ),
        scratch_shapes=[
            pltpu.VMEM((1, REQ), I32),
            pltpu.VMEM((1, REQ), I32),
            pltpu.SemaphoreType.DMA((3,)),
        ],
    )(in_hbm(home.reshape(1, REQ)), in_hbm(item.reshape(1, REQ)), in_hbm(table))
    asked = exchange(wanted.reshape(DEVICES, 1, 128)).reshape(DEVICES, 128)
    picked = call(
        pick_kernel,
        slot_rows,
        "pick",
    )(asked, near_table)
    fetched = exchange(picked)
    own = call(
        own_negatives_kernel,
        shape((OWN_NEG, D), BF16),
        "own_negatives",
        in_specs=[pl.BlockSpec(memory_space=pltpu.SMEM), pl.BlockSpec(memory_space=pl.ANY)],
        scratch_shapes=[
            pltpu.VMEM((OWN_NEG, CAP, D), BF16),
            pltpu.SemaphoreType.DMA((OWN_NEG,)),
        ],
    )(slots, fetched)
    line = spread(own, 0)
    line, speeds = lax.optimization_barrier((line, speeds))
    near = spread(line, 1)
    x, rep, pos_logit = call(
        state_kernel,
        (shape((STEPS, D), BF16), shape((STEPS, D), BF16), shape((STEPS, 1), F32)),
        "state",
        cost=(3 * 10**9, 20 * 2**20),
        grid=over_columns("state"),
        in_specs=[
            whole((1, REQ)),
            slot_columns("state"),
            pl.BlockSpec(memory_space=pltpu.SMEM),
            whole((1, STEPS)),
            whole((STEPS, 1)),
            whole((1, D)),
        ],
        out_specs=(whole((STEPS, D)), whole((STEPS, D)), whole((STEPS, 1))),
        scratch_shapes=[
            pltpu.VMEM((SLOTS, STEPS), BF16),
            pltpu.VMEM((STEPS, STEPS), F32),
            pltpu.VMEM((STEPS, D), F32),
            pltpu.VMEM((STEPS, HEAD_DIM), F32),
        ],
    )(slots, fetched, speeds, forget, forget.reshape(STEPS, 1), gain.reshape(1, D))
    near, x, rep, pos_logit = lax.optimization_barrier((near, x, rep, pos_logit))
    far = swap(near)
    near_logit = call(logits_kernel, shape((STEPS, NEG // 2), F32), "near_logits")(rep, near)
    far, near_logit = lax.optimization_barrier((far, near_logit))
    half_part = shape((NEG // 2, D), BF16)
    loss, d_pos, d_neg, far_part = call(
        loss_kernel,
        (
            shape((STEPS, 1), F32),
            shape((STEPS, 1), F32),
            shape((STEPS, NEG), BF16),
            half_part,
        ),
        "loss",
    )(rep, near_logit, far, pos_logit)
    from_core = swap(far_part)
    near_part = call(near_part_kernel, half_part, "near_part")(d_neg, rep)
    from_core, near_part = lax.optimization_barrier((from_core, near_part))
    near_part = add([near_part, from_core])
    line_part = add(collect(near_part, 1))
    user_grad = call(
        user_grad_kernel,
        shape((1, STEPS, D), BF16),
        "user_grad",
        cost=(10**9, 6 * 2**20),
        grid=over_columns("user_grad"),
        in_specs=[
            columns(STEPS, "user_grad"),
            whole((STEPS, 1)),
            whole((STEPS, NEG)),
            columns(NEG // 2, "user_grad"),
            columns(NEG // 2, "user_grad"),
        ],
        out_specs=pl.BlockSpec((1, STEPS, BLOCK["user_grad"]), lambda j: (0, 0, j)),
    )(x, d_pos, d_neg, near, far)
    asked, d_pos = lax.optimization_barrier((asked, d_pos))
    hot = call(marks_kernel, shape((ITEMS, SLOTS), BF16), "marks", cost=(10**6, 2**20))(asked)
    loss = loss.reshape(1, STEPS)
    user_grad, line_part = lax.optimization_barrier((user_grad, line_part))
    parts = collect(line_part, 0)
    parts, hot, loss = lax.optimization_barrier((parts, hot, loss))
    outgoing = call(
        outgoing_kernel,
        slot_rows,
        "outgoing",
        in_specs=[pl.BlockSpec(memory_space=pltpu.VMEM), pl.BlockSpec(memory_space=pltpu.SMEM)]
        + [pl.BlockSpec(memory_space=pltpu.VMEM)] * 6,
    )(slots, slots, rep, d_pos, *parts)
    arrived = exchange(outgoing)
    item_grad = call(
        place_kernel,
        shape((ITEMS, D), F32),
        "place",
        in_specs=[pl.BlockSpec(memory_space=pltpu.VMEM)] * 2,
        out_specs=pl.BlockSpec(memory_space=pltpu.HBM),
        scratch_shapes=[
            pltpu.VMEM((D // BLOCK["place"], ITEMS, BLOCK["place"]), F32),
            pltpu.SemaphoreType.DMA((D // BLOCK["place"],)),
        ],
    )(hot, arrived)
    return loss, user_grad, item_grad


def solution(mesh):
    return jax.shard_map(
        on_device,
        mesh=mesh,
        in_specs=(
            P(AXES, None),
            P("dp", "seq", None, None),
            P("dp", "seq", None, None),
            P(AXES, None),
            P(AXES, None),
            P(),
        ),
        out_specs=(P(AXES, None), P(AXES, None, None), P(AXES, None)),
        check_vma=False,
    )
```

```python
import jax
import jax.numpy as jnp
from jax import lax
from jax.experimental import pallas as pl
from jax.experimental.pallas import tpu as pltpu
from jax.sharding import PartitionSpec as P

D = 4096
HEADS = 32
HEAD_DIM = 128
STEPS = 256
OWN_NEG = 8
REQ = STEPS + OWN_NEG
NEG = 256
MOVES = 8
ORDER = ((1, 2, 3), (2, 1, 3))
ITEMS = 512
DEVICES = 128
CAP = 4
SLOTS = DEVICES * CAP
SIGMA = 4.0 / 64.0
BLOCK = dict(pick=1024, state=2048, outgoing=1024, user_grad=2048, place=512)
F32 = jnp.float32
BF16 = jnp.bfloat16
I32 = jnp.int32
AXES = ("dp", "seq")


def iota(shape, dim):
    return lax.broadcasted_iota(I32, shape, dim)


def call(kernel, out_shape, name, cost=None, vmem=40, **kw):
    if cost is not None:
        flops, size = cost
        kw["cost_estimate"] = pl.CostEstimate(flops=flops, bytes_accessed=size, transcendentals=0)
    params = pltpu.CompilerParams(vmem_limit_bytes=vmem * 2**20)
    return pl.pallas_call(kernel, out_shape=out_shape, name=name, compiler_params=params, **kw)


def matmul(a, b, dims):
    return lax.dot_general(a, b, ((dims[0], dims[1]), ((), ())), preferred_element_type=F32)


def route_kernel(home, names, table, wanted, slots, near_table, owner_row, item_row, sems):
    first = pltpu.make_async_copy(home, owner_row, sems.at[0])
    second = pltpu.make_async_copy(names, item_row, sems.at[1])
    rows = ITEMS // MOVES
    moves = [
        pltpu.make_async_copy(
            table.at[k * rows : (k + 1) * rows], near_table.at[k * rows : (k + 1) * rows], sems.at[2 + k]
        )
        for k in range(MOVES)
    ]
    first.start()
    second.start()
    for move in moves:
        move.start()
    first.wait()
    second.wait()
    row = owner_row[...]
    same = iota((REQ, REQ), 0) == iota((REQ, REQ), 1)
    col = jnp.sum(jnp.where(same, row.astype(F32), 0.0), axis=1, keepdims=True).astype(I32)

    def key(i):
        return jnp.where(i >= STEPS, i - 2 * STEPS, i)

    earlier = key(iota((REQ, REQ), 0)) < key(iota((REQ, REQ), 1))
    rank = jnp.sum(jnp.where((col == row) & earlier, 1.0, 0.0), axis=0, keepdims=True).astype(I32)
    slots[...] = row * CAP + rank
    item = (item_row[...] + 1).astype(F32)
    here = iota((DEVICES, REQ), 0) == row
    lane = iota((DEVICES, 128), 1)
    out = jnp.full((DEVICES, 128), -1.0, F32)
    for s in range(CAP):
        named = jnp.sum(jnp.where(here & (rank == s), item, 0.0), axis=1, keepdims=True)
        out = jnp.where(lane == s, named - 1.0, out)
    wanted[...] = out.astype(I32)
    for move in moves:
        move.wait()


def onehot_items(asked):
    asked = asked.astype(F32)
    device, slot = iota((DEVICES, SLOTS), 0), iota((DEVICES, SLOTS), 1)
    row = jnp.zeros((DEVICES, SLOTS), F32)
    for s in range(CAP):
        row = row + jnp.where(slot == device * CAP + s, asked[:, s : s + 1], 0.0)
    row = jnp.sum(row, axis=0, keepdims=True)
    return (iota((ITEMS, SLOTS), 0).astype(F32) == row).astype(F32).astype(BF16)


def pick_kernel(asked, table, out):
    hot = onehot_items(asked[...]).astype(F32).T.astype(BF16)
    width = BLOCK["pick"]
    for j in range(0, D, width):
        rows = matmul(hot, table[:, j : j + width], ((1,), (0,)))
        out[:, :, j : j + width] = rows.astype(BF16).reshape(DEVICES, CAP, width)


def marks_kernel(asked, hot):
    hot[...] = onehot_items(asked[...])


def place_kernel(hot, arrived, out, held, sems):
    width = held.shape[2]
    stores = []
    for j in range(D // width):
        part = slice(j * width, (j + 1) * width)
        held[j] = matmul(hot[...], arrived[:, :, part].reshape(SLOTS, width), ((1,), (0,)))
        stores.append(pltpu.make_async_copy(held.at[j], out.at[:, part], sems.at[j]))
        stores[-1].start()
    for store in stores:
        store.wait()


def onehot_slots(slots):
    return (iota((SLOTS, slots.shape[1]), 0) == slots).astype(F32).astype(BF16)


def own_negatives_kernel(slots, rows, out, held, sems):
    copies = []
    for k in range(OWN_NEG):
        owner = slots[0, STEPS + k] // CAP
        copies.append(pltpu.make_async_copy(rows.at[owner], held.at[k], sems.at[k]))
        copies[-1].start()
    total = jnp.zeros(out.shape, F32)
    for k in range(OWN_NEG):
        copies[k].wait()
        rank = slots[0, STEPS + k] % CAP
        tile = jnp.where(iota((CAP, D), 0) == rank, held[k].astype(F32), 0.0)
        row = jnp.sum(tile, axis=0, keepdims=True)
        total = jnp.where(iota(out.shape, 0) == k, row, total)
    out[...] = total.astype(BF16)


def state_kernel(
    slots, rows, speeds, forget_row, forget_col, gain, x_out, rep_out, pos_out, hot, base, prior, total
):
    j, last = pl.program_id(0), pl.num_programs(0) - 1
    width = rows.shape[2]
    heads = width // HEAD_DIM
    step, source = iota((STEPS, STEPS), 0), iota((STEPS, STEPS), 1)

    @pl.when(j == 0)
    def _():
        hot[...] = onehot_slots(slots[:, :STEPS])
        total[...] = jnp.zeros_like(total)
        log_row, log_col = jnp.log(1.0 - forget_row[...]), jnp.log(1.0 - forget_col[...])
        until = jnp.sum(jnp.where(source < step, log_row, 0.0), axis=1, keepdims=True)
        through = jnp.sum(jnp.where(step <= source, log_col, 0.0), axis=0, keepdims=True)
        base[...] = jnp.where(source < step, until - through, -1e30)

    x = matmul(hot[...], rows[...].reshape(SLOTS, width), ((0,), (0,))).astype(BF16)
    x_out[:, pl.ds(pl.multiple_of(j * width, width), width)] = x
    span = (step - 1 - source).astype(F32)
    for k in range(heads):
        full = jnp.exp(base[...] - speeds[0, j * heads + k] * span)
        high = full.astype(BF16)
        low = (full - high.astype(F32)).astype(BF16)
        xk = x[:, k * HEAD_DIM : (k + 1) * HEAD_DIM]
        state = matmul(high, xk, ((1,), (0,))) + matmul(low, xk, ((1,), (0,)))
        total[...] += state * state
        prior[:, pl.ds(pl.multiple_of(j * width + k * HEAD_DIM, HEAD_DIM), HEAD_DIM)] = state

    @pl.when(j == last)
    def _():
        norm = lax.rsqrt(jnp.sum(total[...], axis=1, keepdims=True) * (1.0 / D) + 1e-06)
        pos = jnp.zeros((STEPS, HEAD_DIM), F32)
        for c in range(0, D, HEAD_DIM):
            part = slice(c, c + HEAD_DIM)
            rep = (prior[:, part] * norm * gain[:, part]).astype(BF16)
            rep_out[:, part] = rep
            pos = pos + rep.astype(F32) * x_out[:, part].astype(F32)
        pos_out[...] = SIGMA * jnp.sum(pos, axis=1, keepdims=True)


def logits_kernel(rep, negatives, out):
    out[...] = SIGMA * matmul(rep[...], negatives[...], ((1,), (1,)))


def loss_kernel(rep, near_logit, far, pos_logit, loss, d_pos, d_neg, far_part):
    u = rep[...]
    half = NEG // 2
    logits = [near_logit[...], SIGMA * matmul(u, far[...], ((1,), (1,)))]
    pos = pos_logit[...]
    top = jnp.maximum(jnp.max(jnp.maximum(*logits), axis=1, keepdims=True), pos)
    summed = sum(jnp.sum(jnp.exp(l - top), axis=1, keepdims=True) for l in logits)
    log_total = top + jnp.log(jnp.exp(pos - top) + summed)
    valid = jnp.where(iota((STEPS, 1), 0) > 0, 1.0, 0.0)
    loss[...] = (log_total - pos) * valid
    d_pos[...] = (jnp.exp(pos - log_total) - 1.0) * valid
    shares = [(jnp.exp(l - log_total) * valid).astype(BF16) for l in logits]
    d_neg[:, :half] = shares[0]
    d_neg[:, half:] = shares[1]
    far_part[...] = (SIGMA * matmul(shares[1], u, ((0,), (0,)))).astype(BF16)


def near_part_kernel(d_neg, rep, out):
    out[...] = (SIGMA * matmul(d_neg[:, : NEG // 2], rep[...], ((0,), (0,)))).astype(BF16)


def outgoing_kernel(slots, own_slots, rep, d_pos, *refs):
    *parts, out = refs
    hot = onehot_slots(slots[:, :STEPS])
    width = BLOCK["outgoing"]
    for j in range(0, D, width):
        part = slice(j, j + width)
        grad = (SIGMA * d_pos[...] * rep[:, part].astype(F32)).astype(BF16)
        rows = matmul(hot, grad, ((1,), (0,))).astype(BF16)
        out[:, :, part] = rows.reshape(DEVICES, CAP, width)
    total = sum(p[...].astype(F32) for p in parts).astype(BF16).astype(F32)
    for k in range(OWN_NEG):
        owner, rank = own_slots[0, STEPS + k] // CAP, own_slots[0, STEPS + k] % CAP
        tile = jnp.where(iota((CAP, D), 0) == rank, total[k : k + 1], out[owner].astype(F32))
        out[owner] = tile.astype(BF16)


def user_grad_kernel(x, d_pos, d_neg, near, far, out):
    half = NEG // 2
    from_neg = matmul(d_neg[:, :half], near[...], ((1,), (0,))) + matmul(
        d_neg[:, half:], far[...], ((1,), (0,))
    )
    out[0] = (SIGMA * (d_pos[...] * x[...].astype(F32) + from_neg)).astype(BF16)


def turn(value, stage, by):
    pairs = []
    for x in range(4):
        for y in range(4):
            for c in range(2):
                dx, dy = (by, 0) if (stage + c) % 2 else (0, by)
                to = ((x + dx) % 4 * 4 + (y + dy) % 4) * 2 + c
                pairs.append(((x * 4 + y) * 2 + c, to))
    return lax.ppermute(value, "seq", pairs)


def swap(value):
    return lax.ppermute(value, "seq", [(q, q ^ 1) for q in range(32)])


def spread(rows, stage):
    return jnp.concatenate([rows] + [turn(rows, stage, k) for k in ORDER[stage]], axis=0)


def add(parts):
    return sum(p.astype(F32) for p in parts).astype(BF16)


def collect(rows, stage):
    n = rows.shape[0] // 4
    return [rows[:n]] + [
        turn(rows[k * n : (k + 1) * n], stage, -by) for k, by in enumerate(ORDER[stage], 1)
    ]


def exchange(rows):
    return lax.all_to_all(rows, AXES, split_axis=0, concat_axis=0, tiled=True)


def whole(shape):
    return pl.BlockSpec(shape, lambda j: (0,) * len(shape))


def columns(n, name):
    return pl.BlockSpec((n, BLOCK[name]), lambda j: (0, j))


def slot_columns(name):
    return pl.BlockSpec((DEVICES, CAP, BLOCK[name]), lambda j: (0, 0, j))


def over_columns(name):
    return (D // BLOCK[name],)


def on_device(table, home, item, speeds, forget, gain):
    shape = jax.ShapeDtypeStruct
    slot_rows = shape((DEVICES, CAP, D), BF16)
    in_hbm = lambda a: pltpu.with_memory_space_constraint(a, pltpu.HBM)
    wanted, slots, near_table = call(
        route_kernel,
        (shape((DEVICES, 128), I32), shape((1, REQ), I32), pltpu.VMEM((ITEMS, D), BF16)),
        "route",
        vmem=16,
        in_specs=[pl.BlockSpec(memory_space=pltpu.HBM)] * 3,
        out_specs=(
            pl.BlockSpec(memory_space=pltpu.VMEM),
            pl.BlockSpec(memory_space=pltpu.VMEM),
            pl.BlockSpec(memory_space=pltpu.VMEM),
        ),
        scratch_shapes=[
            pltpu.VMEM((1, REQ), I32),
            pltpu.VMEM((1, REQ), I32),
            pltpu.SemaphoreType.DMA((2 + MOVES,)),
        ],
    )(in_hbm(home.reshape(1, REQ)), in_hbm(item.reshape(1, REQ)), in_hbm(table))
    asked = exchange(wanted.reshape(DEVICES, 1, 128)).reshape(DEVICES, 128)
    picked = call(
        pick_kernel,
        slot_rows,
        "pick",
    )(asked, near_table)
    fetched = exchange(picked)
    own = call(
        own_negatives_kernel,
        shape((OWN_NEG, D), BF16),
        "own_negatives",
        in_specs=[pl.BlockSpec(memory_space=pltpu.SMEM), pl.BlockSpec(memory_space=pl.ANY)],
        scratch_shapes=[
            pltpu.VMEM((OWN_NEG, CAP, D), BF16),
            pltpu.SemaphoreType.DMA((OWN_NEG,)),
        ],
    )(slots, fetched)
    line = spread(own, 0)
    line, speeds = lax.optimization_barrier((line, speeds))
    near = spread(line, 1)
    x, rep, pos_logit = call(
        state_kernel,
        (shape((STEPS, D), BF16), shape((STEPS, D), BF16), shape((STEPS, 1), F32)),
        "state",
        cost=(3 * 10**9, 20 * 2**20),
        grid=over_columns("state"),
        in_specs=[
            whole((1, REQ)),
            slot_columns("state"),
            pl.BlockSpec(memory_space=pltpu.SMEM),
            whole((1, STEPS)),
            whole((STEPS, 1)),
            whole((1, D)),
        ],
        out_specs=(whole((STEPS, D)), whole((STEPS, D)), whole((STEPS, 1))),
        scratch_shapes=[
            pltpu.VMEM((SLOTS, STEPS), BF16),
            pltpu.VMEM((STEPS, STEPS), F32),
            pltpu.VMEM((STEPS, D), F32),
            pltpu.VMEM((STEPS, HEAD_DIM), F32),
        ],
    )(slots, fetched, speeds, forget, forget.reshape(STEPS, 1), gain.reshape(1, D))
    near, x, rep, pos_logit = lax.optimization_barrier((near, x, rep, pos_logit))
    far = swap(near)
    near_logit = call(logits_kernel, shape((STEPS, NEG // 2), F32), "near_logits")(rep, near)
    far, near_logit = lax.optimization_barrier((far, near_logit))
    half_part = shape((NEG // 2, D), BF16)
    loss, d_pos, d_neg, far_part = call(
        loss_kernel,
        (
            shape((STEPS, 1), F32),
            shape((STEPS, 1), F32),
            shape((STEPS, NEG), BF16),
            half_part,
        ),
        "loss",
    )(rep, near_logit, far, pos_logit)
    from_core = swap(far_part)
    near_part = call(near_part_kernel, half_part, "near_part")(d_neg, rep)
    from_core, near_part = lax.optimization_barrier((from_core, near_part))
    near_part = add([near_part, from_core])
    line_part = add(collect(near_part, 1))
    user_grad = call(
        user_grad_kernel,
        shape((1, STEPS, D), BF16),
        "user_grad",
        cost=(10**9, 6 * 2**20),
        grid=over_columns("user_grad"),
        in_specs=[
            columns(STEPS, "user_grad"),
            whole((STEPS, 1)),
            whole((STEPS, NEG)),
            columns(NEG // 2, "user_grad"),
            columns(NEG // 2, "user_grad"),
        ],
        out_specs=pl.BlockSpec((1, STEPS, BLOCK["user_grad"]), lambda j: (0, 0, j)),
    )(x, d_pos, d_neg, near, far)
    asked, d_pos = lax.optimization_barrier((asked, d_pos))
    hot = call(marks_kernel, shape((ITEMS, SLOTS), BF16), "marks", cost=(10**6, 2**20))(asked)
    loss = loss.reshape(1, STEPS)
    user_grad, line_part = lax.optimization_barrier((user_grad, line_part))
    parts = collect(line_part, 0)
    parts, hot, loss = lax.optimization_barrier((parts, hot, loss))
    outgoing = call(
        outgoing_kernel,
        slot_rows,
        "outgoing",
        in_specs=[pl.BlockSpec(memory_space=pltpu.VMEM), pl.BlockSpec(memory_space=pltpu.SMEM)]
        + [pl.BlockSpec(memory_space=pltpu.VMEM)] * 6,
    )(slots, slots, rep, d_pos, *parts)
    arrived = exchange(outgoing)
    item_grad = call(
        place_kernel,
        shape((ITEMS, D), F32),
        "place",
        in_specs=[pl.BlockSpec(memory_space=pltpu.VMEM)] * 2,
        out_specs=pl.BlockSpec(memory_space=pltpu.HBM),
        scratch_shapes=[
            pltpu.VMEM((D // BLOCK["place"], ITEMS, BLOCK["place"]), F32),
            pltpu.SemaphoreType.DMA((D // BLOCK["place"],)),
        ],
    )(hot, arrived)
    return loss, user_grad, item_grad


def solution(mesh):
    return jax.shard_map(
        on_device,
        mesh=mesh,
        in_specs=(
            P(AXES, None),
            P("dp", "seq", None, None),
            P("dp", "seq", None, None),
            P(AXES, None),
            P(AXES, None),
            P(),
        ),
        out_specs=(P(AXES, None), P(AXES, None, None), P(AXES, None)),
        check_vma=False,
    )
```
